256 devices in a mesh: tm: 8 (over y, core), space: 32 (over z, x).
Axes of the slice: x: 4, y: 4, z: 8, core: 2. Of those that a mesh axis runs over, the one named last changes fastest.
Arguments:
- data: bfloat16 [16384, 32768], P('tm', 'space'), may hold values from -70 to 70, as said below
Outputs:
- rfac: float32 [16, 128, 128], replicated
- modes_t: float32 [16, 128, 32768], P(None, None, ('space', 'tm'))
The draws below stay inside these ranges and needn't reach their ends.
Inputs may be any that keep to these rules, and one draw needn't show every extreme that they name: `data`: finite values of order one to some tens.
All inputs are finite; a program needn't handle non-finite values.
Results may differ from the reference program's by a relative error of at most 0.0023.
The reference program's roundings to bfloat16 on the way (of `table`) count: a program that leaves them out, or rounds other values in their place, can miss the bound.
Values may be sent and summed in bfloat16 or wider, within the bound.
A program may use at most 128 MiB of HBM per device.

```python
import jax
import jax.numpy as jnp
from jax import lax

NFFT = 256
NB = 64
F = 16
NT = 16384
NX = 32768


def draw_data(key, part):
    key = jax.random.fold_in(key, 1)
    key_amp, key_freq, key_phase, key_noise = jax.random.split(key, 4)
    amplitude = jnp.exp(jax.random.uniform(key_amp, (NX,), jnp.float32, 0.0, jnp.log(10.0)))
    noise = jax.random.truncated_normal(key_noise, -6.0, 6.0, (NT, NX), jnp.float32)
    bins = jax.random.randint(key_freq, (NX,), 1, F + 1).astype(jnp.float32)
    phase = jax.random.uniform(key_phase, (NX,), jnp.float32, -jnp.pi, jnp.pi)
    within = (jnp.arange(NT, dtype=jnp.int32) % NFFT).astype(jnp.float32)
    angle = within[:, None] * bins[None, :] * (2.0 * jnp.pi / NFFT) + phase[None, :]
    values = amplitude[None, :] * (noise + 0.8 * jnp.cos(angle))
    return values.astype(jnp.bfloat16)


def setup_inputs(seed: int = 0) -> dict:
    seeds = jax.random.split(jax.random.key(seed), 2)
    return {
        "data": draw_data(jax.random.fold_in(seeds[1], 71), 0),
    }


def make_table():
    steps = jnp.arange(NFFT, dtype=jnp.int32)
    window = 0.5 - 0.5 * jnp.cos(2.0 * jnp.pi * steps.astype(jnp.float32) / NFFT)
    factor = 1.0 / jnp.sqrt(jnp.sum(window * window))
    freqs = jnp.arange(1, F + 1, dtype=jnp.int32)
    phases = (steps[:, None] * freqs[None, :] % NFFT).astype(jnp.float32) * (2.0 * jnp.pi / NFFT)
    table = jnp.concatenate([jnp.cos(phases), -jnp.sin(phases)], axis=1) * (factor * window)[:, None]
    return table.astype(jnp.bfloat16)

def reference(data):
    table = make_table()
    colsum = lax.optimization_barrier(jnp.sum(table.astype(jnp.float32), axis=0))
    mean = lax.optimization_barrier(jnp.sum(data, axis=0, dtype=jnp.float32)) / NT
    blocks = data.reshape(NB, NFFT, NX)

    def one_block(block):
        return jnp.dot(table.T.astype(jnp.float32), block.astype(jnp.float32), preferred_element_type=jnp.float32)
    spectra = lax.map(one_block, blocks)
    spectra = spectra - colsum[None, :, None] * mean[None, None, :]
    matrix_t = spectra.reshape(NB, 2, F, NX).transpose(2, 1, 0, 3).reshape(F, 2 * NB, NX)
    gram = jnp.einsum('fcx,fdx->fcd', matrix_t, matrix_t, precision=lax.Precision.HIGHEST) / NX
    lower = jnp.linalg.cholesky(gram)
    modes_t = lax.linalg.triangular_solve(lower, matrix_t, left_side=True, lower=True)
    return (jnp.transpose(lower, (0, 2, 1)), modes_t)
```

```python
import functools

import jax
import jax.numpy as jnp
import ml_dtypes
import numpy as np
from jax import lax
from jax.experimental import pallas as pl
from jax.experimental.pallas import tpu as pltpu
from jax.sharding import PartitionSpec as P

NFFT = 256
NB = 64
F = 16
NT = 16384
NX = 32768
NTM = 8
NSPACE = 32
LB = NB // NTM
COLS = NX // NSPACE
PTS = COLS // NTM
CHUNKS = 4
CW = COLS // CHUNKS
MESH = pl.DeviceIdType.MESH


def make_table():
    steps = np.arange(NFFT)
    window = 0.5 - 0.5 * np.cos(2.0 * np.pi * steps / NFFT)
    factor = 1.0 / np.sqrt(np.sum(window * window))
    freqs = np.arange(1, F + 1)
    phases = (steps[:, None] * freqs[None, :] % NFFT) * (2.0 * np.pi / NFFT)
    real = np.cos(phases) * (factor * window)[:, None]
    imag = -np.sin(phases) * (factor * window)[:, None]
    pairs = np.stack([real.T, imag.T], axis=1).reshape(2 * F, NFFT)
    rounded = pairs.astype(np.float32).astype(ml_dtypes.bfloat16)
    colsum = rounded.astype(np.float32).sum(axis=1, dtype=np.float32)
    rows = np.zeros((48, NFFT), ml_dtypes.bfloat16)
    rows[: 2 * F] = rounded
    rows[2 * F] = 1.0
    return rows, colsum


def factor(gt_ref, w_ref):
    lane = lax.broadcasted_iota(jnp.int32, (8, 128), 1)
    sub = lax.broadcasted_iota(jnp.int32, (8, 128), 0)
    for j in range(16):
        w_ref[j] = gt_ref[j]
    for k in range(16):
        base = 8 * k
        own = w_ref[k]
        cols = [jnp.broadcast_to(own[:, base + i : base + i + 1], (8, 128)) for i in range(8)]
        pivot_rows, inverses, cross = [], [], []
        diag = jnp.ones((8, 128), jnp.float32)
        for i in range(8):
            d = jnp.broadcast_to(cols[i][i : i + 1, :], (8, 128))
            inv = 1.0 / d
            row = jnp.broadcast_to(own[i : i + 1, :], (8, 128))
            diag = jnp.where(sub == i, d, diag)
            f = jnp.where(sub > i, cols[i] * inv, 0.0)
            here = [jnp.broadcast_to(cols[m][i : i + 1, :], (8, 128)) for m in range(i + 1, 8)]
            for n, m in enumerate(range(i + 1, 8)):
                cols[m] = cols[m] - f * here[n]
            unit = jnp.where(lane == base + i, 1.0, row)
            own = jnp.where((lane == base + i) & (sub > i), 0.0, own) - f * unit
            pivot_rows.append(jnp.where((lane > base + i) & (lane < base + 8), 0.0, unit))
            inverses.append(inv)
            cross.append(here)
        w_ref[k] = own * lax.rsqrt(diag)
        for j in range(k + 1, 16):
            rest = w_ref[j]
            mult = [jnp.broadcast_to(rest[:, base + i : base + i + 1], (8, 128)) for i in range(8)]
            rest = jnp.where((lane >= base) & (lane < base + 8), 0.0, rest)
            for i in range(8):
                f = mult[i] * inverses[i]
                for n, m in enumerate(range(i + 1, 8)):
                    mult[m] = mult[m] - f * cross[i][n]
                rest = rest - f * pivot_rows[i]
            w_ref[j] = rest


def main_kernel(
    data, tab, cs, wa, mf,
    dbuf, spec, sb, rb, ls, mat, gs, gr, gt, w,
    load_sem, fs_sem, fr_sem, ls_ssem, ls_rsem, ps_sem, pr_sem,
    ga_ssem, ga_rsem, gb_ssem, gb_rsem, w_ssem, w_rsem, own_sem,
):
    t = lax.axis_index("tm")
    s = lax.axis_index("space")
    z, x = s // 4, s % 4
    h = x % 2
    tile = (x // 2) * 8 + z
    pair = z * 4 + (x // 2) * 2

    loads = []
    for c in range(CHUNKS):
        copy = pltpu.make_async_copy(
            data.at[:, pl.ds(c * CW, CW)], dbuf.at[c], load_sem.at[c]
        )
        copy.start()
        loads.append(copy)

    barrier = pltpu.get_barrier_semaphore()

    def greet_tm(k, carry):
        other = (t + k) % NTM
        pl.semaphore_signal(barrier, inc=1, device_id=(other, s), device_id_type=MESH)
        pl.semaphore_signal(
            barrier, inc=1, device_id=(other, pair + 1 - h), device_id_type=MESH
        )
        return carry

    def greet_space(k, carry):
        pl.semaphore_signal(
            barrier, inc=1, device_id=(t, (s + k) % NSPACE), device_id_type=MESH
        )
        return carry

    lax.fori_loop(1, NTM, greet_tm, 0)
    lax.fori_loop(1, NSPACE, greet_space, 0)

    def freq_copy(c, other):
        cols = pl.ds(c * CW, CW)
        return pltpu.make_async_remote_copy(
            src_ref=sb.at[pl.ds(2 * other, 2), :, cols],
            dst_ref=rb.at[:, pl.ds(t * 16, 16), cols],
            send_sem=fs_sem.at[c, other],
            recv_sem=fr_sem.at[c, t],
            device_id=(other, s),
            device_id_type=MESH,
        )

    for c in range(CHUNKS):
        cols = pl.ds(c * CW, CW)
        loads[c].wait()
        total = jnp.zeros((1, CW), jnp.float32)
        for b in range(LB):
            out = jnp.dot(
                tab[...], dbuf[c, pl.ds(b * NFFT, NFFT), :], preferred_element_type=jnp.float32
            )
            for r in range(CW // 128):
                spec[c * (CW // 128) + r, pl.ds(b, 2 * F, stride=LB), :] = out[
                    : 2 * F, r * 128 : (r + 1) * 128
                ]
            total = total + out[2 * F : 2 * F + 1]
        for r in range(CW // 128):
            ls[t, pl.ds(c * (CW // 128) + r, 1), :] = total[:, r * 128 : (r + 1) * 128]
        local_mean = jnp.broadcast_to(total * (NTM / NT), (LB, CW))
        for r in range(CW // 128):
            place = c * (CW // 128) + r
            for f in range(F):
                parts = [
                    spec[place, pl.ds(f * 16 + ri * 8, 8), :]
                    - cs[2 * f + ri] * local_mean[:, r * 128 : (r + 1) * 128]
                    for ri in range(2)
                ]
                sb[f, :, pl.ds(place * 128, 128)] = jnp.concatenate(parts, axis=0).astype(
                    jnp.bfloat16
                )
        if c == 0:
            pl.semaphore_wait(barrier, 2 * (NTM - 1) + NSPACE - 1)

        def send(k, carry):
            freq_copy(c, (t + k) % NTM).start()
            return carry

        lax.fori_loop(1, NTM, send, 0)

    def sum_copy(other):
        return pltpu.make_async_remote_copy(
            src_ref=ls.at[t],
            dst_ref=ls.at[t],
            send_sem=ls_ssem.at[other],
            recv_sem=ls_rsem.at[t],
            device_id=(other, s),
            device_id_type=MESH,
        )

    def send_sums(k, carry):
        sum_copy((t + k) % NTM).start()
        return carry

    lax.fori_loop(1, NTM, send_sums, 0)
    for f2 in range(2):
        rb[f2, pl.ds(t * 16, 16), :] = sb[2 * t + f2]

    def recv_sums(k, carry):
        other = (t + k) % NTM
        pltpu.make_async_remote_copy(
            src_ref=ls.at[t],
            dst_ref=ls.at[other],
            send_sem=ls_ssem.at[other],
            recv_sem=ls_rsem.at[other],
            device_id=(other, s),
            device_id_type=MESH,
        ).wait()
        return carry

    lax.fori_loop(1, NTM, recv_sums, 0)
    mean = ls[0]
    for k in range(1, NTM):
        mean = mean + ls[k]
    mean = mean * (1.0 / NT)

    def subtract(f, carry):
        for ri in range(2):
            rows = pl.ds(pl.multiple_of(f * 16 + ri * 8, 8), 8)
            for r in range(8):
                spec[r, rows, :] = spec[r, rows, :] - cs[2 * f + ri] * mean[r : r + 1, :]
        return carry

    lax.fori_loop(0, F, subtract, 0)

    def point_copy(other):
        return pltpu.make_async_remote_copy(
            src_ref=spec5.at[other],
            dst_ref=mf.at[:, :, t],
            send_sem=ps_sem.at[other],
            recv_sem=pr_sem.at[t],
            device_id=(other, s),
            device_id_type=MESH,
        )

    spec5 = spec.reshape(NTM, F, 2, LB, PTS)

    def send_points(k, carry):
        point_copy((t + k) % NTM).start()
        return carry

    lax.fori_loop(1, NTM, send_points, 0)
    own_points = pltpu.make_async_copy(
        spec5.at[t], mf.at[:, :, t], own_sem
    )
    own_points.start()

    def recv_freq(k, carry):
        other = (t + k) % NTM
        for c in range(CHUNKS):
            cols = pl.ds(c * CW, CW)
            pltpu.make_async_remote_copy(
                src_ref=sb.at[pl.ds(2 * other, 2), :, cols],
                dst_ref=rb.at[:, pl.ds(other * 16, 16), cols],
                send_sem=fs_sem.at[c, other],
                recv_sem=fr_sem.at[c, other],
                device_id=(other, s),
                device_id_type=MESH,
            ).wait()
        return carry

    lax.fori_loop(1, NTM, recv_freq, 0)
    for f2 in range(2):
        real, imag = cs[4 * t + 2 * f2], cs[4 * t + 2 * f2 + 1]

        def gather(k, carry):
            shift = ls[k] * (NTM / NT) - mean
            for r in range(8):
                lanes = pl.ds(r * 128, 128)
                block = rb[f2, pl.ds(pl.multiple_of(k * 16, 16), 16), lanes].astype(jnp.float32)
                row = jnp.broadcast_to(shift[r : r + 1, :], (8, 128))
                mat[pl.ds(pl.multiple_of(k * 8, 8), 8), lanes] = block[:8] + real * row
                mat[pl.ds(pl.multiple_of(64 + k * 8, 8), 8), lanes] = block[8:] + imag * row
            return carry

        lax.fori_loop(0, NTM, gather, 0)
        rounded = mat[...].astype(jnp.bfloat16)
        gram = lax.dot_general(
            rounded, rounded, (((1,), (1,)), ((), ())), preferred_element_type=jnp.float32
        ) * (1.0 / NX)
        for i in range(16):
            gs[f2, i] = gram[i * 8 : (i + 1) * 8]

    def gram_copy(k):
        other = (s + k) % NSPACE
        ox, oz = other % 4, other // 4
        return pltpu.make_async_remote_copy(
            src_ref=gs.at[ox % 2, (ox // 2) * 8 + oz],
            dst_ref=gr.at[s],
            send_sem=ga_ssem.at[other],
            recv_sem=ga_rsem.at[s],
            device_id=(t, other),
            device_id_type=MESH,
        )

    def send_gram(k, carry):
        gram_copy(k).start()
        return carry

    lax.fori_loop(1, NSPACE, send_gram, 0)
    gr[s] = gs[h, tile]

    def recv_gram(k, carry):
        other = (s + k) % NSPACE
        ox, oz = other % 4, other // 4
        pltpu.make_async_remote_copy(
            src_ref=gs.at[ox % 2, (ox // 2) * 8 + oz],
            dst_ref=gr.at[other],
            send_sem=ga_ssem.at[other],
            recv_sem=ga_rsem.at[other],
            device_id=(t, other),
            device_id_type=MESH,
        ).wait()
        return carry

    lax.fori_loop(1, NSPACE, recv_gram, 0)
    rows = gr[0]
    for k in range(1, NSPACE):
        rows = rows + gr[k]
    gt[tile] = rows

    def tile_copy(k, landing):
        other = (tile + k) % 16
        ox, oz = (other // 8) * 2 + h, other % 8
        return pltpu.make_async_remote_copy(
            src_ref=gt.at[tile],
            dst_ref=gt.at[other if landing else tile],
            send_sem=gb_ssem.at[other],
            recv_sem=gb_rsem.at[other if landing else tile],
            device_id=(t, oz * 4 + ox),
            device_id_type=MESH,
        )

    def send_tile(k, carry):
        tile_copy(k, False).start()
        return carry

    def recv_tile(k, carry):
        tile_copy(k, True).wait()
        return carry

    lax.fori_loop(1, 16, send_tile, 0)
    lax.fori_loop(1, 16, recv_tile, 0)

    factor(gt, w)

    mine = 2 * t + h

    def factor_copy(k, landing):
        other = (mine + k) % F
        return pltpu.make_async_remote_copy(
            src_ref=w,
            dst_ref=wa.at[other if landing else mine],
            send_sem=w_ssem.at[other],
            recv_sem=w_rsem.at[other if landing else mine],
            device_id=(other // 2, pair + other % 2),
            device_id_type=MESH,
        )

    def send_factor(k, carry):
        factor_copy(k, False).start()
        return carry

    def recv_factor(k, carry):
        factor_copy(k, True).wait()
        return carry

    lax.fori_loop(1, F, send_factor, 0)
    own_factor = pltpu.make_async_copy(w, wa.at[mine], own_sem)
    own_points.wait()
    own_factor.start()

    def recv_points(k, carry):
        other = (t + k) % NTM
        pltpu.make_async_remote_copy(
            src_ref=spec5.at[other],
            dst_ref=mf.at[:, :, other],
            send_sem=ps_sem.at[other],
            recv_sem=pr_sem.at[other],
            device_id=(other, s),
            device_id_type=MESH,
        ).wait()
        return carry

    lax.fori_loop(1, NTM, recv_points, 0)
    lax.fori_loop(1, F, recv_factor, 0)
    own_factor.wait()


def modes_kernel(w, m, rfac, modes):
    row = lax.broadcasted_iota(jnp.int32, (128, 128), 0)
    col = lax.broadcasted_iota(jnp.int32, (128, 128), 1)
    packed = w[0]
    rfac[0] = jnp.where(col >= row, packed, 0.0)
    inverse = jnp.where(col < row, packed, jnp.where(col == row, 1.0 / packed, 0.0))
    modes[0] = jnp.dot(
        inverse, m[0], preferred_element_type=jnp.float32, precision=lax.Precision.HIGH
    )


def shards(data):
    rows, colsum = make_table()
    f32, bf16 = jnp.float32, jnp.bfloat16
    dma = pltpu.SemaphoreType.DMA
    vmem = pltpu.VMEM
    packed, points = pl.pallas_call(
        main_kernel,
        out_shape=(
            jax.ShapeDtypeStruct((F, 16, 8, 128), f32),
            jax.ShapeDtypeStruct((F, 2, NTM, LB, PTS), f32),
        ),
        in_specs=[
            pl.BlockSpec(memory_space=pl.ANY),
            pl.BlockSpec(memory_space=pltpu.VMEM),
            pl.BlockSpec(memory_space=pltpu.SMEM),
        ],
        out_specs=[pl.BlockSpec(memory_space=pl.ANY), pl.BlockSpec(memory_space=pl.ANY)],
        scratch_shapes=[
            vmem((CHUNKS, NT // NTM, CW), bf16),
            vmem((NTM, 2 * F * LB, PTS), f32),
            vmem((F, 2 * LB, COLS), bf16),
            vmem((2, 2 * NB, COLS), bf16),
            vmem((NTM, 8, 128), f32),
            vmem((2 * NB, COLS), f32),
            vmem((2, 16, 8, 128), f32),
            vmem((NSPACE, 8, 128), f32),
            vmem((16, 8, 128), f32),
            vmem((16, 8, 128), f32),
            dma((CHUNKS,)),
            dma((CHUNKS, NTM)),
            dma((CHUNKS, NTM)),
            dma((NTM,)),
            dma((NTM,)),
            dma((NTM,)),
            dma((NTM,)),
            dma((NSPACE,)),
            dma((NSPACE,)),
            dma((16,)),
            dma((16,)),
            dma((F,)),
            dma((F,)),
            dma,
        ],
        compiler_params=pltpu.CompilerParams(
            collective_id=0, has_side_effects=True, vmem_limit_bytes=32 * 1024 * 1024
        ),
        name="factors",
    )(data, jnp.asarray(rows), jnp.asarray(colsum))
    spec = pl.BlockSpec((1, 128, 128), lambda f: (f, 0, 0))
    return pl.pallas_call(
        modes_kernel,
        grid=(F,),
        out_shape=(
            jax.ShapeDtypeStruct((F, 128, 128), f32),
            jax.ShapeDtypeStruct((F, 128, PTS), f32),
        ),
        in_specs=[spec, spec],
        out_specs=[spec, spec],
        name="modes",
    )(packed.reshape(F, 128, 128), points.reshape(F, 128, PTS))


def solution(mesh):
    return jax.shard_map(
        shards,
        mesh=mesh,
        in_specs=(P("tm", "space"),),
        out_specs=(P(), P(None, None, ("space", "tm"))),
        check_vma=False,
    )
```

```python
import functools

import jax
import jax.numpy as jnp
import ml_dtypes
import numpy as np
from jax import lax
from jax.experimental import pallas as pl
from jax.experimental.pallas import tpu as pltpu
from jax.sharding import PartitionSpec as P

NFFT = 256
NB = 64
F = 16
NT = 16384
NX = 32768
NTM = 8
NSPACE = 32
LB = NB // NTM
COLS = NX // NSPACE
PTS = COLS // NTM
CHUNKS = 4
CW = COLS // CHUNKS
MESH = pl.DeviceIdType.MESH


def make_table():
    steps = np.arange(NFFT)
    window = 0.5 - 0.5 * np.cos(2.0 * np.pi * steps / NFFT)
    factor = 1.0 / np.sqrt(np.sum(window * window))
    freqs = np.arange(1, F + 1)
    phases = (steps[:, None] * freqs[None, :] % NFFT) * (2.0 * np.pi / NFFT)
    real = np.cos(phases) * (factor * window)[:, None]
    imag = -np.sin(phases) * (factor * window)[:, None]
    pairs = np.stack([real.T, imag.T], axis=1).reshape(2 * F, NFFT)
    rounded = pairs.astype(np.float32).astype(ml_dtypes.bfloat16)
    colsum = rounded.astype(np.float32).sum(axis=1, dtype=np.float32)
    rows = np.zeros((48, NFFT), ml_dtypes.bfloat16)
    rows[: 2 * F] = rounded
    rows[2 * F] = 1.0
    return rows, colsum


def factor(gt_ref, w_ref):
    lane = lax.broadcasted_iota(jnp.int32, (8, 128), 1)
    sub = lax.broadcasted_iota(jnp.int32, (8, 128), 0)
    for j in range(16):
        w_ref[j] = gt_ref[j]
    for k in range(16):
        base = 8 * k
        own = w_ref[k]
        cols = [jnp.broadcast_to(own[:, base + i : base + i + 1], (8, 128)) for i in range(8)]
        pivot_rows, inverses, cross = [], [], []
        diag = jnp.ones((8, 128), jnp.float32)
        for i in range(8):
            d = jnp.broadcast_to(cols[i][i : i + 1, :], (8, 128))
            inv = 1.0 / d
            row = jnp.broadcast_to(own[i : i + 1, :], (8, 128))
            diag = jnp.where(sub == i, d, diag)
            f = jnp.where(sub > i, cols[i] * inv, 0.0)
            here = [jnp.broadcast_to(cols[m][i : i + 1, :], (8, 128)) for m in range(i + 1, 8)]
            for n, m in enumerate(range(i + 1, 8)):
                cols[m] = cols[m] - f * here[n]
            unit = jnp.where(lane == base + i, 1.0, row)
            own = jnp.where((lane == base + i) & (sub > i), 0.0, own) - f * unit
            pivot_rows.append(jnp.where((lane > base + i) & (lane < base + 8), 0.0, unit))
            inverses.append(inv)
            cross.append(here)
        w_ref[k] = own * lax.rsqrt(diag)
        for j in range(k + 1, 16):
            rest = w_ref[j]
            mult = [jnp.broadcast_to(rest[:, base + i : base + i + 1], (8, 128)) for i in range(8)]
            rest = jnp.where((lane >= base) & (lane < base + 8), 0.0, rest)
            for i in range(8):
                f = mult[i] * inverses[i]
                for n, m in enumerate(range(i + 1, 8)):
                    mult[m] = mult[m] - f * cross[i][n]
                rest = rest - f * pivot_rows[i]
            w_ref[j] = rest


def plane_distance(dz, dx):
    return min(dz, 8 - dz) + min(dx, 4 - dx)


PLANE = sorted(
    [(dz, dx) for dz in range(8) for dx in range(4) if dz or dx],
    key=lambda o: -plane_distance(*o),
)
HALF = [o for o in PLANE if o[1] % 2 == 0]
GROUP = [(2, 0), (2, 1), (1, 0), (3, 0), (1, 1), (3, 1), (0, 1)]
SHARE = [(2, 1), (2, 0), (1, 1), (3, 1), (1, 0), (3, 0), (0, 1)]


def main_kernel(
    colsum,
    data, tab_hbm, rfac, modes,
    tab, cs, dbuf, spec, sb, rb, ls, mat, gs, gr, gt, w, wa, mf,
    tab_sem, load_sem, fs_sem, fr_sem, ls_ssem, ls_rsem, ps_sem, pr_sem,
    ga_ssem, ga_rsem, gb_ssem, gb_rsem, w_ssem, w_rsem, r_ssem, r_rsem, own_sem,
):
    t = lax.axis_index("tm")
    s = lax.axis_index("space")
    y, core = t // 2, t % 2
    z, x = s // 4, s % 4
    h = x % 2
    tile = (x // 2) * 8 + z
    pair = z * 4 + (x // 2) * 2
    sibling = 2 * y + 1 - core

    load_tab = pltpu.make_async_copy(tab_hbm, tab, tab_sem)
    load_tab.start()
    loads = []
    for c in range(CHUNKS):
        copy = pltpu.make_async_copy(
            data.at[:, pl.ds(c * CW, CW)], dbuf.at[c], load_sem.at[c]
        )
        copy.start()
        loads.append(copy)

    def remote(src, dst, send_sem, recv_sem, device):
        return pltpu.make_async_remote_copy(
            src_ref=src,
            dst_ref=dst,
            send_sem=send_sem,
            recv_sem=recv_sem,
            device_id=device,
            device_id_type=MESH,
        )

    def group_peer(o):
        return ((y + o[0]) % 4) * 2 + (core + o[1]) % 2

    def group_source(o):
        return ((y + 4 - o[0]) % 4) * 2 + (core + o[1]) % 2

    def plane_peer(o):
        return ((z + o[0]) % 8) * 4 + (x + o[1]) % 4

    barrier = pltpu.get_barrier_semaphore()
    for o in PLANE:
        pl.semaphore_signal(barrier, inc=1, device_id=(t, plane_peer(o)), device_id_type=MESH)
    for o in GROUP:
        pl.semaphore_signal(barrier, inc=1, device_id=(group_peer(o), s), device_id_type=MESH)
    for o in GROUP:
        pl.semaphore_signal(
            barrier, inc=1, device_id=(group_peer(o), pair + 1 - h), device_id_type=MESH
        )

    for j in range(2 * F):
        cs[j] = jnp.float32(colsum[j])
    load_tab.wait()
    table = tab[...].astype(jnp.bfloat16)
    sends = []

    for c in range(CHUNKS):
        cols = pl.ds(c * CW, CW)
        loads[c].wait()
        total = jnp.zeros((1, CW), jnp.float32)
        for b in range(LB):
            out = jnp.dot(
                table, dbuf[c, pl.ds(b * NFFT, NFFT), :], preferred_element_type=jnp.float32
            )
            for r in range(CW // 128):
                spec[c * (CW // 128) + r, pl.ds(b, 2 * F, stride=LB), :] = out[
                    : 2 * F, r * 128 : (r + 1) * 128
                ]
            total = total + out[2 * F : 2 * F + 1]
        for r in range(CW // 128):
            ls[t, pl.ds(c * (CW // 128) + r, 1), :] = total[:, r * 128 : (r + 1) * 128]
        local_mean = jnp.broadcast_to(total * (NTM / NT), (LB, CW))
        for r in range(CW // 128):
            place = c * (CW // 128) + r
            for f in range(F):
                parts = [
                    spec[place, pl.ds(f * 16 + ri * 8, 8), :]
                    - colsum[2 * f + ri] * local_mean[:, r * 128 : (r + 1) * 128]
                    for ri in range(2)
                ]
                sb[f, :, pl.ds(place * 128, 128)] = jnp.concatenate(parts, axis=0).astype(
                    jnp.bfloat16
                )
        if c == 0:
            pl.semaphore_wait(barrier, 2 * len(GROUP) + len(PLANE))
        for i, o in enumerate(GROUP):
            other = group_peer(o)
            copy = remote(
                sb.at[pl.ds(2 * other, 2), :, cols],
                rb.at[:, pl.ds(pl.multiple_of(t * 16, 16), 16), cols],
                fs_sem.at[c, i],
                fr_sem.at[c, i],
                (other, s),
            )
            copy.start()
            sends.append(copy)

    for i, o in enumerate(GROUP):
        copy = remote(ls.at[t], ls.at[t], ls_ssem.at[i], ls_rsem.at[i], (group_peer(o), s))
        copy.start()
        sends.append(copy)
    for f2 in range(2):
        rb[f2, pl.ds(pl.multiple_of(t * 16, 16), 16), :] = sb[2 * t + f2]

    for i, o in enumerate(GROUP):
        source = group_source(o)
        remote(
            ls.at[t], ls.at[source], ls_ssem.at[i], ls_rsem.at[i], (source, s)
        ).wait_recv()
    mean = ls[0]
    for k in range(1, NTM):
        mean = mean + ls[k]
    mean = mean * (1.0 / NT)

    def subtract(f, carry):
        for ri in range(2):
            rows = pl.ds(pl.multiple_of(f * 16 + ri * 8, 8), 8)
            for r in range(8):
                spec[r, rows, :] = spec[r, rows, :] - cs[2 * f + ri] * mean[r : r + 1, :]
        return carry

    lax.fori_loop(0, F, subtract, 0)
    spec5 = spec.reshape(NTM, F, 2, LB, PTS)
    for i, o in enumerate(GROUP):
        other = group_peer(o)
        copy = remote(spec5.at[other], mf.at[:, :, t], ps_sem.at[i], pr_sem.at[i], (other, s))
        copy.start()
        sends.append(copy)
    own_points = pltpu.make_async_copy(spec5.at[t], mf.at[:, :, t], own_sem)
    own_points.start()

    for i, o in enumerate(GROUP):
        source = group_source(o)
        for c in range(CHUNKS):
            cols = pl.ds(c * CW, CW)
            remote(
                sb.at[pl.ds(2 * source, 2), :, cols],
                rb.at[:, pl.ds(pl.multiple_of(source * 16, 16), 16), cols],
                fs_sem.at[c, i],
                fr_sem.at[c, i],
                (source, s),
            ).wait_recv()
    for f2 in range(2):
        real, imag = cs[4 * t + 2 * f2], cs[4 * t + 2 * f2 + 1]

        def gather(k, carry):
            shift = ls[k] * (NTM / NT) - mean
            for r in range(8):
                lanes = pl.ds(r * 128, 128)
                block = rb[f2, pl.ds(pl.multiple_of(k * 16, 16), 16), lanes].astype(jnp.float32)
                row = jnp.broadcast_to(shift[r : r + 1, :], (8, 128))
                mat[pl.ds(pl.multiple_of(k * 8, 8), 8), lanes] = block[:8] + real * row
                mat[pl.ds(pl.multiple_of(64 + k * 8, 8), 8), lanes] = block[8:] + imag * row
            return carry

        lax.fori_loop(0, NTM, gather, 0)
        rounded = mat[...].astype(jnp.bfloat16)
        gram = lax.dot_general(
            rounded, rounded, (((1,), (1,)), ((), ())), preferred_element_type=jnp.float32
        ) * (1.0 / NX)
        for i in range(16):
            gs[f2, i] = gram[i * 8 : (i + 1) * 8]

    for i, o in enumerate(PLANE):
        oz, ox = (z + o[0]) % 8, (x + o[1]) % 4
        copy = remote(
            gs.at[ox % 2, (ox // 2) * 8 + oz],
            gr.at[i],
            ga_ssem.at[i],
            ga_rsem.at[i],
            (t, oz * 4 + ox),
        )
        copy.start()
        sends.append(copy)
    rows = gs[h, tile]
    for i in reversed(range(len(PLANE))):
        remote(gs.at[0, 0], gr.at[i], ga_ssem.at[i], ga_rsem.at[i], (t, s)).wait_recv()
        rows = rows + gr[i]
    gt[tile] = rows

    for i, o in enumerate(HALF):
        copy = remote(
            gt.at[tile], gt.at[tile], gb_ssem.at[i], gb_rsem.at[i], (t, plane_peer(o))
        )
        copy.start()
        sends.append(copy)
    for i, o in enumerate(HALF):
        oz, ox = (z + 8 - o[0]) % 8, (x + o[1]) % 4
        source = (ox // 2) * 8 + oz
        remote(
            gt.at[tile], gt.at[source], gb_ssem.at[i], gb_rsem.at[i], (t, oz * 4 + ox)
        ).wait_recv()

    factor(gt, w)

    mine = 2 * t + h
    for i, o in enumerate(SHARE):
        peer = (((y + o[0]) % 4) * 2 + core, pair + (h + o[1]) % 2)
        copy = remote(w, wa.at[mine], w_ssem.at[i], w_rsem.at[i], peer)
        copy.start()
        sends.append(copy)
    copy = remote(w, wa.at[mine], r_ssem.at[7], r_rsem.at[7], (sibling, s))
    copy.start()
    sends.append(copy)
    own_points.wait()
    for i, o in enumerate(GROUP):
        source = group_source(o)
        remote(
            spec5.at[source], mf.at[:, :, source], ps_sem.at[i], pr_sem.at[i], (source, s)
        ).wait_recv()
    row = lax.broadcasted_iota(jnp.int32, (128, 128), 0)
    col = lax.broadcasted_iota(jnp.int32, (128, 128), 1)

    def multiply(f, packed):
        packed = packed.reshape(128, 128)
        rfac[f] = jnp.where(col >= row, packed, 0.0)
        inverse = jnp.where(col < row, packed, jnp.where(col == row, 1.0 / packed, 0.0))
        modes[f] = jnp.dot(
            inverse,
            mf[f].reshape(128, PTS),
            preferred_element_type=jnp.float32,
            precision=lax.Precision.HIGH,
        )

    multiply(mine, w[...])
    for i in reversed(range(len(SHARE))):
        o = SHARE[i]
        f = 4 * ((y + 4 - o[0]) % 4) + 2 * core + (h + o[1]) % 2
        remote(w, wa.at[f], w_ssem.at[i], w_rsem.at[i], (sibling, s)).wait_recv()
        copy = remote(wa.at[f], wa.at[f], r_ssem.at[i], r_rsem.at[i], (sibling, s))
        copy.start()
        sends.append(copy)
        multiply(f, wa[f])
    for i in reversed(range(len(SHARE) + 1)):
        o = SHARE[i] if i < len(SHARE) else (0, 0)
        f = 4 * ((y + 4 - o[0]) % 4) + 2 * (1 - core) + (h + o[1]) % 2
        remote(w, wa.at[f], r_ssem.at[i], r_rsem.at[i], (sibling, s)).wait_recv()
        multiply(f, wa[f])
    for copy in sends:
        copy.wait_send()


def hand_out(rfac, modes, rfac_out, modes_out, sems):
    copies = [
        pltpu.make_async_copy(rfac, rfac_out, sems.at[0]),
        pltpu.make_async_copy(modes, modes_out, sems.at[1]),
    ]
    for copy in copies:
        copy.start()
    for copy in copies:
        copy.wait()


def shards(data):
    rows, colsum = make_table()
    f32, bf16 = jnp.float32, jnp.bfloat16
    dma = pltpu.SemaphoreType.DMA
    vmem = pltpu.VMEM
    rfac, modes = pl.pallas_call(
        functools.partial(main_kernel, [float(v) for v in colsum]),
        out_shape=(vmem((F, 128, 128), f32), vmem((F, 128, PTS), f32)),
        in_specs=[pl.BlockSpec(memory_space=pltpu.HBM), pl.BlockSpec(memory_space=pltpu.HBM)],
        out_specs=[pl.BlockSpec(memory_space=pltpu.VMEM), pl.BlockSpec(memory_space=pltpu.VMEM)],
        scratch_shapes=[
            vmem((48, NFFT), f32),
            pltpu.SMEM((2 * F,), f32),
            vmem((CHUNKS, NT // NTM, CW), bf16),
            vmem((NTM, 2 * F * LB, PTS), f32),
            vmem((F, 2 * LB, COLS), bf16),
            vmem((2, 2 * NB, COLS), bf16),
            vmem((NTM, 8, 128), f32),
            vmem((2 * NB, COLS), f32),
            vmem((2, 16, 8, 128), f32),
            vmem((NSPACE, 8, 128), f32),
            vmem((16, 8, 128), f32),
            vmem((16, 8, 128), f32),
            vmem((F, 16, 8, 128), f32),
            vmem((F, 2, NTM, LB, PTS), f32),
            dma,
            dma((CHUNKS,)),
            dma((CHUNKS, 7)),
            dma((CHUNKS, 7)),
            dma((7,)),
            dma((7,)),
            dma((7,)),
            dma((7,)),
            dma((NSPACE,)),
            dma((NSPACE,)),
            dma((16,)),
            dma((16,)),
            dma((7,)),
            dma((7,)),
            dma((8,)),
            dma((8,)),
            dma,
        ],
        compiler_params=pltpu.CompilerParams(
            collective_id=0, has_side_effects=True, vmem_limit_bytes=56 * 1024 * 1024
        ),
        name="factors",
    )(data, jnp.asarray(rows.astype(np.float32)))
    return pl.pallas_call(
        hand_out,
        out_shape=(
            jax.ShapeDtypeStruct((F, 128, 128), f32),
            jax.ShapeDtypeStruct((F, 128, PTS), f32),
        ),
        in_specs=[pl.BlockSpec(memory_space=pltpu.VMEM), pl.BlockSpec(memory_space=pltpu.VMEM)],
        out_specs=[pl.BlockSpec(memory_space=pl.ANY), pl.BlockSpec(memory_space=pl.ANY)],
        scratch_shapes=[dma((2,))],
        compiler_params=pltpu.CompilerParams(vmem_limit_bytes=8 * 1024 * 1024),
        name="hand_out",
    )(rfac, modes)


def solution(mesh):
    return jax.shard_map(
        shards,
        mesh=mesh,
        in_specs=(P("tm", "space"),),
        out_specs=(P(), P(None, None, ("space", "tm"))),
        check_vma=False,
    )
```

```python
import functools

import jax
import jax.numpy as jnp
import ml_dtypes
import numpy as np
from jax import lax
from jax.experimental import pallas as pl
from jax.experimental.pallas import tpu as pltpu
from jax.sharding import PartitionSpec as P

NFFT = 256
NB = 64
F = 16
NT = 16384
NX = 32768
NTM = 8
NSPACE = 32
LB = NB // NTM
COLS = NX // NSPACE
PTS = COLS // NTM
CHUNKS = 4
CW = COLS // CHUNKS
MESH = pl.DeviceIdType.MESH


def make_table():
    steps = np.arange(NFFT)
    window = 0.5 - 0.5 * np.cos(2.0 * np.pi * steps / NFFT)
    factor = 1.0 / np.sqrt(np.sum(window * window))
    freqs = np.arange(1, F + 1)
    phases = (steps[:, None] * freqs[None, :] % NFFT) * (2.0 * np.pi / NFFT)
    real = np.cos(phases) * (factor * window)[:, None]
    imag = -np.sin(phases) * (factor * window)[:, None]
    pairs = np.stack([real.T, imag.T], axis=1).reshape(2 * F, NFFT)
    rounded = pairs.astype(np.float32).astype(ml_dtypes.bfloat16)
    colsum = rounded.astype(np.float32).sum(axis=1, dtype=np.float32)
    rows = np.zeros((48, NFFT), ml_dtypes.bfloat16)
    rows[: 2 * F] = rounded
    rows[2 * F] = 1.0
    return rows, colsum


def factor(gt_ref, w_ref):
    lane = lax.broadcasted_iota(jnp.int32, (8, 128), 1)
    sub = lax.broadcasted_iota(jnp.int32, (8, 128), 0)
    for j in range(16):
        w_ref[j] = gt_ref[j]
    for k in range(16):
        base = 8 * k
        own = w_ref[k]
        cols = [jnp.broadcast_to(own[:, base + i : base + i + 1], (8, 128)) for i in range(8)]
        pivot_rows, inverses, cross = [], [], []
        diag = jnp.ones((8, 128), jnp.float32)
        for i in range(8):
            d = jnp.broadcast_to(cols[i][i : i + 1, :], (8, 128))
            inv = 1.0 / d
            row = jnp.broadcast_to(own[i : i + 1, :], (8, 128))
            diag = jnp.where(sub == i, d, diag)
            f = jnp.where(sub > i, cols[i] * inv, 0.0)
            here = [jnp.broadcast_to(cols[m][i : i + 1, :], (8, 128)) for m in range(i + 1, 8)]
            for n, m in enumerate(range(i + 1, 8)):
                cols[m] = cols[m] - f * here[n]
            unit = jnp.where(lane == base + i, 1.0, row)
            own = jnp.where((lane == base + i) & (sub > i), 0.0, own) - f * unit
            pivot_rows.append(jnp.where((lane > base + i) & (lane < base + 8), 0.0, unit))
            inverses.append(inv)
            cross.append(here)
        w_ref[k] = own * lax.rsqrt(diag)
        for j in range(k + 1, 16):
            rest = w_ref[j]
            mult = [jnp.broadcast_to(rest[:, base + i : base + i + 1], (8, 128)) for i in range(8)]
            rest = jnp.where((lane >= base) & (lane < base + 8), 0.0, rest)
            for i in range(8):
                f = mult[i] * inverses[i]
                for n, m in enumerate(range(i + 1, 8)):
                    mult[m] = mult[m] - f * cross[i][n]
                rest = rest - f * pivot_rows[i]
            w_ref[j] = rest


def plane_distance(dz, dx):
    return min(dz, 8 - dz) + min(dx, 4 - dx)


PLANE = sorted(
    [(dz, dx) for dz in range(8) for dx in range(4) if dz or dx],
    key=lambda o: -plane_distance(*o),
)
OFFSET_Y = (1, 3, 2, 0, 1, 3, 2)
HALF = [o for o in PLANE if sum(o) % 2 == 0]
OTHER = [o for o in PLANE if sum(o) % 2 == 1]
GROUP = [(2, 0), (2, 1), (1, 0), (3, 0), (1, 1), (3, 1), (0, 1)]


def main_kernel(
    colsum,
    data, tab_hbm, rfac, modes,
    tab, cs, dbuf, spec, sb, rb, ls, mat, gs, gr, gt, w, wa, mf,
    tab_sem, load_sem, fs_sem, fr_sem, ls_ssem, ls_rsem, ps_sem, pr_sem,
    ga_ssem, ga_rsem, gb_ssem, gb_rsem, w_ssem, w_rsem, r_ssem, r_rsem, own_sem,
    group_in, plane_in,
):
    t = lax.axis_index("tm")
    s = lax.axis_index("space")
    y, core = t // 2, t % 2
    z, x = s // 4, s % 4
    h = (x + z) % 2
    tile = z * 2 + x // 2
    sibling = 2 * y + 1 - core

    load_tab = pltpu.make_async_copy(tab_hbm, tab, tab_sem)
    load_tab.start()
    loads = []
    for c in range(CHUNKS):
        copy = pltpu.make_async_copy(
            data.at[:, pl.ds(c * CW, CW)], dbuf.at[c], load_sem.at[c]
        )
        copy.start()
        loads.append(copy)

    def remote(src, dst, send_sem, recv_sem, device):
        return pltpu.make_async_remote_copy(
            src_ref=src,
            dst_ref=dst,
            send_sem=send_sem,
            recv_sem=recv_sem,
            device_id=device,
            device_id_type=MESH,
        )

    def group_peer(o):
        return ((y + o[0]) % 4) * 2 + (core + o[1]) % 2

    def group_source(o):
        return ((y + 4 - o[0]) % 4) * 2 + (core + o[1]) % 2

    def plane_peer(o):
        return ((z + o[0]) % 8) * 4 + (x + o[1]) % 4

    barrier = pltpu.get_barrier_semaphore()

    def signal(sem, device):
        pl.semaphore_signal(sem, inc=1, device_id=device, device_id_type=MESH)

    for dy in range(4):
        other = ((y + dy) % 4) * 2
        if dy == 0:

            @pl.when(core == 1)
            def _():
                signal(barrier, (other, s))

        else:
            signal(barrier, (other, s))

    for j in range(2 * F):
        cs[j] = jnp.float32(colsum[j])
    load_tab.wait()
    table = tab[...].astype(jnp.bfloat16)
    sends = []

    for c in range(CHUNKS):
        cols = pl.ds(c * CW, CW)
        loads[c].wait()
        total = jnp.zeros((1, CW), jnp.float32)
        for b in range(LB):
            out = jnp.dot(
                table, dbuf[c, pl.ds(b * NFFT, NFFT), :], preferred_element_type=jnp.float32
            )
            for r in range(CW // 128):
                spec[c * (CW // 128) + r, pl.ds(b, 2 * F, stride=LB), :] = out[
                    : 2 * F, r * 128 : (r + 1) * 128
                ]
            total = total + out[2 * F : 2 * F + 1]
        for r in range(CW // 128):
            ls[t, pl.ds(c * (CW // 128) + r, 1), :] = total[:, r * 128 : (r + 1) * 128]
        local_mean = jnp.broadcast_to(total * (NTM / NT), (LB, CW))
        for r in range(CW // 128):
            place = c * (CW // 128) + r
            for f in range(F):
                parts = [
                    spec[place, pl.ds(f * 16 + ri * 8, 8), :]
                    - colsum[2 * f + ri] * local_mean[:, r * 128 : (r + 1) * 128]
                    for ri in range(2)
                ]
                sb[f, :, pl.ds(place * 128, 128)] = jnp.concatenate(parts, axis=0).astype(
                    jnp.bfloat16
                )

    @pl.when(core == 0)
    def _():
        pl.semaphore_wait(barrier, len(GROUP))
        signal(group_in, (sibling, s))

    @pl.when(core == 1)
    def _():
        pl.semaphore_wait(group_in, 1)

    for i, o in enumerate(GROUP):
        copy = remote(ls.at[t], ls.at[t], ls_ssem.at[i], ls_rsem.at[i], (group_peer(o), s))
        copy.start()
        sends.append(copy)
    for f2 in range(2):
        for i, o in enumerate(GROUP):
            other = group_peer(o)
            copy = remote(
                sb.at[2 * other + f2],
                rb.at[f2, pl.ds(pl.multiple_of(t * 16, 16), 16), :],
                fs_sem.at[f2, i],
                fr_sem.at[f2, i],
                (other, s),
            )
            copy.start()
            sends.append(copy)

    @pl.when(core == 1)
    def _():
        for o in PLANE:
            signal(barrier, (t, plane_peer(o)))

    for f2 in range(2):
        rb[f2, pl.ds(pl.multiple_of(t * 16, 16), 16), :] = sb[2 * t + f2]

    for i, o in enumerate(GROUP):
        source = group_source(o)
        remote(
            ls.at[t], ls.at[source], ls_ssem.at[i], ls_rsem.at[i], (source, s)
        ).wait_recv()
    mean = ls[0]
    for k in range(1, NTM):
        mean = mean + ls[k]
    mean = mean * (1.0 / NT)

    def subtract(f, carry):
        for ri in range(2):
            rows = pl.ds(pl.multiple_of(f * 16 + ri * 8, 8), 8)
            for r in range(8):
                spec[r, rows, :] = spec[r, rows, :] - cs[2 * f + ri] * mean[r : r + 1, :]
        return carry

    lax.fori_loop(0, F, subtract, 0)
    spec5 = spec.reshape(NTM, F, 2, LB, PTS)

    for f2 in range(2):
        for i, o in enumerate(GROUP):
            source = group_source(o)
            remote(
                sb.at[source],
                rb.at[f2, pl.ds(pl.multiple_of(source * 16, 16), 16), :],
                fs_sem.at[f2, i],
                fr_sem.at[f2, i],
                (source, s),
            ).wait_recv()
        real, imag = cs[4 * t + 2 * f2], cs[4 * t + 2 * f2 + 1]

        def gather(k, carry):
            shift = ls[k] * (NTM / NT) - mean
            for r in range(8):
                lanes = pl.ds(r * 128, 128)
                block = rb[f2, pl.ds(pl.multiple_of(k * 16, 16), 16), lanes].astype(jnp.float32)
                row = jnp.broadcast_to(shift[r : r + 1, :], (8, 128))
                mat[pl.ds(pl.multiple_of(k * 8, 8), 8), lanes] = block[:8] + real * row
                mat[pl.ds(pl.multiple_of(64 + k * 8, 8), 8), lanes] = block[8:] + imag * row
            return carry

        lax.fori_loop(0, NTM, gather, 0)
        rounded = mat[...].astype(jnp.bfloat16)
        gram = lax.dot_general(
            rounded, rounded, (((1,), (1,)), ((), ())), preferred_element_type=jnp.float32
        ) * (1.0 / NX)
        for i in range(16):
            gs[f2, i] = gram[i * 8 : (i + 1) * 8]

        if f2 == 0:

            @pl.when(core == 1)
            def _():
                pl.semaphore_wait(barrier, len(PLANE))
                signal(plane_in, (sibling, s))

            @pl.when(core == 0)
            def _():
                pl.semaphore_wait(plane_in, 1)

        change = (h + f2) % 2

        def choose(a, b):
            return jnp.where(change == 0, a, b)

        def send_rows(i):
            keep = HALF[min(i, len(HALF) - 1)]
            oz = (z + choose(keep[0], OTHER[i][0])) % 8
            ox = (x + choose(keep[1], OTHER[i][1])) % 4
            k = choose(PLANE.index(keep), PLANE.index(OTHER[i]))
            remote(
                gs.at[f2, oz * 2 + ox // 2],
                gr.at[k],
                ga_ssem.at[k],
                ga_rsem.at[k],
                (t, oz * 4 + ox),
            ).start()

        for i in range(len(HALF)):
            send_rows(i)

        @pl.when(change == 1)
        def _():
            send_rows(len(HALF))

        if f2 == 0:
            for i, o in enumerate(GROUP):
                other = group_peer(o)
                copy = remote(
                    spec5.at[other], mf.at[:, :, t], ps_sem.at[i], pr_sem.at[i], (other, s)
                )
                copy.start()
                sends.append(copy)
            own_points = pltpu.make_async_copy(spec5.at[t], mf.at[:, :, t], own_sem)
            own_points.start()

    rows = gs[h, tile]
    for i in reversed(range(len(PLANE))):
        remote(gs.at[0, 0], gr.at[i], ga_ssem.at[i], ga_rsem.at[i], (t, s)).wait_recv()
        rows = rows + gr[i]
    gt[tile] = rows

    for i, o in enumerate(HALF):
        copy = remote(
            gt.at[tile], gt.at[tile], gb_ssem.at[i], gb_rsem.at[i], (t, plane_peer(o))
        )
        copy.start()
        sends.append(copy)
    for i, o in enumerate(HALF):
        oz, ox = (z + 8 - o[0]) % 8, (x + 4 - o[1]) % 4
        source = oz * 2 + ox // 2
        remote(
            gt.at[tile], gt.at[source], gb_ssem.at[i], gb_rsem.at[i], (t, oz * 4 + ox)
        ).wait_recv()

    factor(gt, w)

    mine = 2 * t + h
    for slot in (2, 6, 5, 4, 1, 0, 3):
        dy = OFFSET_Y[slot]
        other_y = (y + dy) % 4
        if slot < 3:
            column = s
        else:
            d = (y + other_y) % 4
            dx = jnp.where(d == 0, 1, jnp.where(d == 1, 3, 0))
            dz = jnp.where(d == 2, 1, jnp.where(d == 3, 7, 0))
            column = ((z + dz) % 8) * 4 + (x + dx) % 4
        copy = remote(
            w, wa.at[mine], w_ssem.at[slot], w_rsem.at[slot], (other_y * 2 + core, column)
        )
        copy.start()
        sends.append(copy)
    copy = remote(w, wa.at[mine], r_ssem.at[7], r_rsem.at[7], (sibling, s))
    copy.start()
    sends.append(copy)
    own_points.wait()
    for i, o in enumerate(GROUP):
        source = group_source(o)
        remote(
            spec5.at[source], mf.at[:, :, source], ps_sem.at[i], pr_sem.at[i], (source, s)
        ).wait_recv()
    row = lax.broadcasted_iota(jnp.int32, (128, 128), 0)
    col = lax.broadcasted_iota(jnp.int32, (128, 128), 1)

    def multiply(f, packed):
        packed = packed.reshape(128, 128)
        rfac[f] = jnp.where(col >= row, packed, 0.0)
        inverse = jnp.where(col < row, packed, jnp.where(col == row, 1.0 / packed, 0.0))
        modes[f] = jnp.dot(
            inverse,
            mf[f].reshape(128, PTS),
            preferred_element_type=jnp.float32,
            precision=lax.Precision.HIGH,
        )

    multiply(mine, w[...])
    order = [(i + 3 * h) % 7 for i in range(7)]

    def frequency(slot, of_core):
        turn = slot % 7
        dy = jnp.where(
            turn < 3,
            jnp.where(turn == 2, 2, 1 + 2 * turn),
            jnp.where(turn == 6, 2, jnp.where(turn == 5, 3, turn - 3)),
        )
        half = jnp.where(turn < 3, h, 1 - h)
        return 4 * ((y + 4 - dy) % 4) + 2 * of_core + half

    for slot in order:
        f = frequency(slot, core)
        remote(w, wa.at[f], w_ssem.at[slot], w_rsem.at[slot], (sibling, s)).wait_recv()
        copy = remote(wa.at[f], wa.at[f], r_ssem.at[slot], r_rsem.at[slot], (sibling, s))
        copy.start()
        sends.append(copy)
        multiply(f, wa[f])
    for i in range(8):
        slot = order[i - 1] if i else 7
        f = frequency(slot, 1 - core) if i else 4 * y + 2 * (1 - core) + h
        remote(w, wa.at[f], r_ssem.at[slot], r_rsem.at[slot], (sibling, s)).wait_recv()
        multiply(f, wa[f])
    for k in range(len(PLANE)):
        remote(gs.at[0, 0], gr.at[k], ga_ssem.at[k], ga_rsem.at[k], (t, s)).wait_send()
    for copy in sends:
        copy.wait_send()


def hand_out(rfac, modes, rfac_out, modes_out, sems):
    copies = [
        pltpu.make_async_copy(rfac, rfac_out, sems.at[0]),
        pltpu.make_async_copy(modes, modes_out, sems.at[1]),
    ]
    for copy in copies:
        copy.start()
    for copy in copies:
        copy.wait()


def shards(data):
    rows, colsum = make_table()
    f32, bf16 = jnp.float32, jnp.bfloat16
    dma = pltpu.SemaphoreType.DMA
    vmem = pltpu.VMEM
    rfac, modes = pl.pallas_call(
        functools.partial(main_kernel, [float(v) for v in colsum]),
        out_shape=(vmem((F, 128, 128), f32), vmem((F, 128, PTS), f32)),
        in_specs=[pl.BlockSpec(memory_space=pltpu.HBM), pl.BlockSpec(memory_space=pltpu.HBM)],
        out_specs=[pl.BlockSpec(memory_space=pltpu.VMEM), pl.BlockSpec(memory_space=pltpu.VMEM)],
        scratch_shapes=[
            vmem((48, NFFT), f32),
            pltpu.SMEM((2 * F,), f32),
            vmem((CHUNKS, NT // NTM, CW), bf16),
            vmem((NTM, 2 * F * LB, PTS), f32),
            vmem((F, 2 * LB, COLS), bf16),
            vmem((2, 2 * NB, COLS), bf16),
            vmem((NTM, 8, 128), f32),
            vmem((2 * NB, COLS), f32),
            vmem((2, 16, 8, 128), f32),
            vmem((NSPACE, 8, 128), f32),
            vmem((16, 8, 128), f32),
            vmem((16, 8, 128), f32),
            vmem((F, 16, 8, 128), f32),
            vmem((F, 2, NTM, LB, PTS), f32),
            dma,
            dma((CHUNKS,)),
            dma((2, 7)),
            dma((2, 7)),
            dma((7,)),
            dma((7,)),
            dma((7,)),
            dma((7,)),
            dma((NSPACE,)),
            dma((NSPACE,)),
            dma((16,)),
            dma((16,)),
            dma((7,)),
            dma((7,)),
            dma((8,)),
            dma((8,)),
            dma,
            pltpu.SemaphoreType.REGULAR,
            pltpu.SemaphoreType.REGULAR,
        ],
        compiler_params=pltpu.CompilerParams(
            collective_id=0, has_side_effects=True, vmem_limit_bytes=56 * 1024 * 1024
        ),
        name="factors",
    )(data, jnp.asarray(rows.astype(np.float32)))
    return pl.pallas_call(
        hand_out,
        out_shape=(
            jax.ShapeDtypeStruct((F, 128, 128), f32),
            jax.ShapeDtypeStruct((F, 128, PTS), f32),
        ),
        in_specs=[pl.BlockSpec(memory_space=pltpu.VMEM), pl.BlockSpec(memory_space=pltpu.VMEM)],
        out_specs=[pl.BlockSpec(memory_space=pl.ANY), pl.BlockSpec(memory_space=pl.ANY)],
        scratch_shapes=[dma((2,))],
        compiler_params=pltpu.CompilerParams(vmem_limit_bytes=8 * 1024 * 1024),
        name="hand_out",
    )(rfac, modes)


def solution(mesh):
    return jax.shard_map(
        shards,
        mesh=mesh,
        in_specs=(P("tm", "space"),),
        out_specs=(P(), P(None, None, ("space", "tm"))),
        check_vma=False,
    )
```

```python
import functools

import jax
import jax.numpy as jnp
import ml_dtypes
import numpy as np
from jax import lax
from jax.experimental import pallas as pl
from jax.experimental.pallas import tpu as pltpu
from jax.sharding import PartitionSpec as P

NFFT = 256
NB = 64
F = 16
NT = 16384
NX = 32768
NTM = 8
NSPACE = 32
LB = NB // NTM
COLS = NX // NSPACE
PTS = COLS // NTM
CHUNKS = 4
CW = COLS // CHUNKS
MESH = pl.DeviceIdType.MESH


def make_table():
    steps = np.arange(NFFT)
    window = 0.5 - 0.5 * np.cos(2.0 * np.pi * steps / NFFT)
    factor = 1.0 / np.sqrt(np.sum(window * window))
    freqs = np.arange(1, F + 1)
    phases = (steps[:, None] * freqs[None, :] % NFFT) * (2.0 * np.pi / NFFT)
    real = np.cos(phases) * (factor * window)[:, None]
    imag = -np.sin(phases) * (factor * window)[:, None]
    pairs = np.stack([real.T, imag.T], axis=1).reshape(2 * F, NFFT)
    rounded = pairs.astype(np.float32).astype(ml_dtypes.bfloat16)
    colsum = rounded.astype(np.float32).sum(axis=1, dtype=np.float32)
    rows = np.zeros((48, NFFT), ml_dtypes.bfloat16)
    rows[: 2 * F] = rounded
    rows[2 * F] = 1.0
    return rows, colsum


def factor(gt_ref, w_ref, half_done):
    lane = lax.broadcasted_iota(jnp.int32, (8, 128), 1)
    sub = lax.broadcasted_iota(jnp.int32, (8, 128), 0)
    for j in range(16):
        w_ref[j] = gt_ref[j]
    for k in range(16):
        base = 8 * k
        own = w_ref[k]
        cols = [jnp.broadcast_to(own[:, base + i : base + i + 1], (8, 128)) for i in range(8)]
        pivot_rows, inverses, cross = [], [], []
        diag = jnp.ones((8, 128), jnp.float32)
        for i in range(8):
            d = jnp.broadcast_to(cols[i][i : i + 1, :], (8, 128))
            inv = 1.0 / d
            row = jnp.broadcast_to(own[i : i + 1, :], (8, 128))
            diag = jnp.where(sub == i, d, diag)
            f = cols[i] * inv
            here = [jnp.broadcast_to(cols[m][i : i + 1, :], (8, 128)) for m in range(i + 1, 8)]
            for n, m in enumerate(range(i + 1, 8)):
                cols[m] = cols[m] - f * here[n]
            unit = jnp.where(lane == base + i, 1.0, row)
            own = jnp.where((lane == base + i) & (sub > i), 0.0, own) - jnp.where(
                sub > i, f, 0.0
            ) * unit
            pivot_rows.append(jnp.where((lane > base + i) & (lane < base + 8), 0.0, unit))
            inverses.append(inv)
            cross.append(here)
        w_ref[k] = own * lax.rsqrt(diag)
        if k == 7:
            half_done()
        for j in range(k + 1, 16):
            rest = w_ref[j]
            mult = [jnp.broadcast_to(rest[:, base + i : base + i + 1], (8, 128)) for i in range(8)]
            rest = jnp.where((lane >= base) & (lane < base + 8), 0.0, rest)
            for i in range(8):
                f = mult[i] * inverses[i]
                for n, m in enumerate(range(i + 1, 8)):
                    mult[m] = mult[m] - f * cross[i][n]
                rest = rest - f * pivot_rows[i]
            w_ref[j] = rest


def plane_distance(dz, dx):
    return min(dz, 8 - dz) + min(dx, 4 - dx)


PLANE = sorted(
    [(dz, dx) for dz in range(8) for dx in range(4) if dz or dx],
    key=lambda o: -plane_distance(*o),
)
OFFSET_Y = (1, 3, 2, 0, 1, 3, 2)
HALF = [o for o in PLANE if sum(o) % 2 == 0]
OTHER = [o for o in PLANE if sum(o) % 2 == 1]
GROUP = [(2, 0), (2, 1), (1, 0), (3, 0), (1, 1), (3, 1), (0, 1)]


def main_kernel(
    colsum,
    data, tab_hbm, rfac, modes,
    tab, cs, dbuf, spec, sb, rb, ls, mat, gs, gr, gt, w, wa, mf,
    tab_sem, load_sem, fs_sem, ls_sem, ps_sem, ga_sem, gb_sem,
    w_ssem, w_rsem, r_ssem, r_rsem, own_sem, group_in, plane_in,
):
    t = lax.axis_index("tm")
    s = lax.axis_index("space")
    y, core = t // 2, t % 2
    z, x = s // 4, s % 4
    h = (x + z) % 2
    tile = z * 2 + x // 2
    sibling = 2 * y + 1 - core

    load_tab = pltpu.make_async_copy(tab_hbm, tab, tab_sem)
    load_tab.start()
    loads = []
    for c in range(CHUNKS):
        copy = pltpu.make_async_copy(
            data.at[:, pl.ds(c * CW, CW)], dbuf.at[c], load_sem.at[c]
        )
        copy.start()
        loads.append(copy)

    def remote(src, dst, send_sem, recv_sem, device):
        return pltpu.make_async_remote_copy(
            src_ref=src,
            dst_ref=dst,
            send_sem=send_sem,
            recv_sem=recv_sem,
            device_id=device,
            device_id_type=MESH,
        )

    def group_peer(o):
        return ((y + o[0]) % 4) * 2 + (core + o[1]) % 2

    def group_source(o):
        return ((y + 4 - o[0]) % 4) * 2 + (core + o[1]) % 2

    def plane_peer(o):
        return ((z + o[0]) % 8) * 4 + (x + o[1]) % 4

    barrier = pltpu.get_barrier_semaphore()

    def signal(sem, device):
        pl.semaphore_signal(sem, inc=1, device_id=device, device_id_type=MESH)

    for dy in range(4):
        other = ((y + dy) % 4) * 2
        if dy == 0:

            @pl.when(core == 1)
            def _():
                signal(barrier, (other, s))

        else:
            signal(barrier, (other, s))

    for j in range(2 * F):
        cs[j] = jnp.float32(colsum[j])
    load_tab.wait()
    table = tab[...].astype(jnp.bfloat16)

    for c in range(CHUNKS):
        cols = pl.ds(c * CW, CW)
        loads[c].wait()
        total = jnp.zeros((1, CW), jnp.float32)
        for b in range(LB):
            out = jnp.dot(
                table, dbuf[c, pl.ds(b * NFFT, NFFT), :], preferred_element_type=jnp.float32
            )
            for r in range(CW // 128):
                spec[c * (CW // 128) + r, pl.ds(b, 2 * F, stride=LB), :] = out[
                    : 2 * F, r * 128 : (r + 1) * 128
                ]
            total = total + out[2 * F : 2 * F + 1]
        for r in range(CW // 128):
            ls[t, pl.ds(c * (CW // 128) + r, 1), :] = total[:, r * 128 : (r + 1) * 128]
        local_mean = jnp.broadcast_to(total * (NTM / NT), (LB, CW))
        for r in range(CW // 128):
            place = c * (CW // 128) + r
            for f in range(F):
                parts = [
                    spec[place, pl.ds(f * 16 + ri * 8, 8), :]
                    - colsum[2 * f + ri] * local_mean[:, r * 128 : (r + 1) * 128]
                    for ri in range(2)
                ]
                sb[f, :, pl.ds(place * 128, 128)] = jnp.concatenate(parts, axis=0).astype(
                    jnp.bfloat16
                )

    @pl.when(core == 0)
    def _():
        pl.semaphore_wait(barrier, len(GROUP))
        signal(group_in, (sibling, s))

    @pl.when(core == 1)
    def _():
        pl.semaphore_wait(group_in, 1)

    def all_of(ref, send_sem, recv_sem):
        return remote(ref, ref, send_sem, recv_sem, (sibling, s))

    for o in GROUP:
        remote(ls.at[t], ls.at[t], ls_sem.at[0], ls_sem.at[1], (group_peer(o), s)).start()
    for f2 in range(2):
        for o in GROUP:
            other = group_peer(o)
            remote(
                sb.at[2 * other + f2],
                rb.at[f2, pl.ds(pl.multiple_of(t * 16, 16), 16), :],
                fs_sem.at[0],
                fs_sem.at[1 + f2],
                (other, s),
            ).start()

    @pl.when(core == 1)
    def _():
        for o in PLANE:
            signal(barrier, (t, plane_peer(o)))

    for f2 in range(2):
        rb[f2, pl.ds(pl.multiple_of(t * 16, 16), 16), :] = sb[2 * t + f2]

    sums_done = all_of(ls.at[pl.ds(0, 7)], ls_sem.at[0], ls_sem.at[1])
    sums_done.wait_recv()
    mean = ls[0]
    for k in range(1, NTM):
        mean = mean + ls[k]
    mean = mean * (1.0 / NT)

    def subtract(f, carry):
        for ri in range(2):
            rows = pl.ds(pl.multiple_of(f * 16 + ri * 8, 8), 8)
            for r in range(8):
                spec[r, rows, :] = spec[r, rows, :] - cs[2 * f + ri] * mean[r : r + 1, :]
        return carry

    lax.fori_loop(0, F, subtract, 0)
    spec5 = spec.reshape(NTM, F, 2, LB, PTS)

    for f2 in range(2):
        all_of(rb.at[f2, pl.ds(0, 7 * 16)], fs_sem.at[0], fs_sem.at[1 + f2]).wait_recv()
        real, imag = cs[4 * t + 2 * f2], cs[4 * t + 2 * f2 + 1]

        def gather(k, carry):
            shift = ls[k] * (NTM / NT) - mean
            for r in range(8):
                lanes = pl.ds(r * 128, 128)
                block = rb[f2, pl.ds(pl.multiple_of(k * 16, 16), 16), lanes].astype(jnp.float32)
                row = jnp.broadcast_to(shift[r : r + 1, :], (8, 128))
                mat[pl.ds(pl.multiple_of(k * 8, 8), 8), lanes] = block[:8] + real * row
                mat[pl.ds(pl.multiple_of(64 + k * 8, 8), 8), lanes] = block[8:] + imag * row
            return carry

        lax.fori_loop(0, NTM, gather, 0)
        rounded = mat[...].astype(jnp.bfloat16)
        gram = lax.dot_general(
            rounded, rounded, (((1,), (1,)), ((), ())), preferred_element_type=jnp.float32
        ) * (1.0 / NX)
        for i in range(16):
            gs[f2, i] = gram[i * 8 : (i + 1) * 8]

        if f2 == 0:

            @pl.when(core == 1)
            def _():
                pl.semaphore_wait(barrier, len(PLANE))
                signal(plane_in, (sibling, s))

            @pl.when(core == 0)
            def _():
                pl.semaphore_wait(plane_in, 1)

        change = (h + f2) % 2

        def choose(a, b):
            return jnp.where(change == 0, a, b)

        def send_rows(i):
            keep = HALF[min(i, len(HALF) - 1)]
            oz = (z + choose(keep[0], OTHER[i][0])) % 8
            ox = (x + choose(keep[1], OTHER[i][1])) % 4
            k = choose(PLANE.index(keep), PLANE.index(OTHER[i]))
            remote(
                gs.at[f2, oz * 2 + ox // 2],
                gr.at[k],
                ga_sem.at[0],
                ga_sem.at[1],
                (t, oz * 4 + ox),
            ).start()

        for i in range(len(HALF)):
            send_rows(i)

        @pl.when(change == 1)
        def _():
            send_rows(len(HALF))

        if f2 == 0:
            for o in GROUP:
                other = group_peer(o)
                remote(
                    spec5.at[other], mf.at[:, :, t], ps_sem.at[0], ps_sem.at[1], (other, s)
                ).start()
            own_points = pltpu.make_async_copy(spec5.at[t], mf.at[:, :, t], own_sem)
            own_points.start()

    rows = gs[h, tile]
    rows_done = all_of(gr.at[pl.ds(0, len(PLANE))], ga_sem.at[0], ga_sem.at[1])
    rows_done.wait_recv()
    for i in range(len(PLANE)):
        rows = rows + gr[i]
    gt[tile] = rows

    for o in HALF:
        remote(gt.at[tile], gt.at[tile], gb_sem.at[0], gb_sem.at[1], (t, plane_peer(o))).start()
    tiles_done = all_of(gt.at[pl.ds(0, len(HALF))], gb_sem.at[0], gb_sem.at[1])
    tiles_done.wait_recv()

    mine = 2 * t + h

    def send_half(part):
        half_rows = pl.ds(8 * part, 8)
        for slot in (2, 1, 0, 6, 5, 4, 3):
            dy = OFFSET_Y[slot]
            other_y = (y + dy) % 4
            if slot < 3:
                column = s
            else:
                d = (y + other_y) % 4
                dx = jnp.where(d == 0, 1, jnp.where(d == 1, 3, 0))
                dz = jnp.where(d == 2, 1, jnp.where(d == 3, 7, 0))
                column = ((z + dz) % 8) * 4 + (x + dx) % 4
            remote(
                w.at[half_rows],
                wa.at[mine, half_rows],
                w_ssem,
                w_rsem.at[part, slot],
                (other_y * 2 + core, column),
            ).start()
        remote(
            w.at[half_rows], wa.at[mine, half_rows], r_ssem, r_rsem.at[part, 7], (sibling, s)
        ).start()

    factor(gt, w, lambda: send_half(0))
    send_half(1)
    own_points.wait()
    points_done = all_of(mf.at[:, :, pl.ds(0, 7)], ps_sem.at[0], ps_sem.at[1])
    points_done.wait_recv()
    row = lax.broadcasted_iota(jnp.int32, (128, 128), 0)
    col = lax.broadcasted_iota(jnp.int32, (128, 128), 1)

    def multiply(f, packed):
        packed = packed.reshape(128, 128)
        rfac[f] = jnp.where(col >= row, packed, 0.0)
        inverse = jnp.where(col < row, packed, jnp.where(col == row, 1.0 / packed, 0.0))
        modes[f] = jnp.dot(
            inverse,
            mf[f].reshape(128, PTS),
            preferred_element_type=jnp.float32,
            precision=lax.Precision.HIGH,
        )

    multiply(mine, w[...])
    order = [(i + 3 * h) % 7 for i in range(7)]

    def frequency(slot, of_core):
        turn = slot % 7
        dy = jnp.where(
            turn < 3,
            jnp.where(turn == 2, 2, 1 + 2 * turn),
            jnp.where(turn == 6, 2, jnp.where(turn == 5, 3, turn - 3)),
        )
        half = jnp.where(turn < 3, h, 1 - h)
        return 4 * ((y + 4 - dy) % 4) + 2 * of_core + half

    def relay(slot, part):
        f = frequency(slot, core)
        half_rows = wa.at[f, pl.ds(8 * part, 8)]
        remote(half_rows, half_rows, w_ssem, w_rsem.at[part, slot], (sibling, s)).wait_recv()
        remote(half_rows, half_rows, r_ssem, r_rsem.at[part, slot], (sibling, s)).start()

    for slots in (order[:3], order[3:]):
        for slot in slots:
            relay(slot, 0)
        for slot in slots:
            relay(slot, 1)
            f = frequency(slot, core)
            multiply(f, wa[f])
    for i in range(8):
        slot = order[i - 1] if i else 7
        f = frequency(slot, 1 - core) if i else 4 * y + 2 * (1 - core) + h
        for part in range(2):
            half_rows = wa.at[f, pl.ds(8 * part, 8)]
            remote(half_rows, half_rows, r_ssem, r_rsem.at[part, slot], (sibling, s)).wait_recv()
        multiply(f, wa[f])

    for done in (sums_done, rows_done, tiles_done, points_done):
        done.wait_send()
    all_of(sb.at[pl.ds(0, 14)], fs_sem.at[0], fs_sem.at[1]).wait_send()
    all_of(wa.at[pl.ds(0, 7)], w_ssem, w_ssem).wait_send()
    all_of(wa.at[pl.ds(0, 8)], r_ssem, r_ssem).wait_send()


def hand_out(rfac, modes, rfac_out, modes_out, sems):
    copies = [
        pltpu.make_async_copy(rfac, rfac_out, sems.at[0]),
        pltpu.make_async_copy(modes, modes_out, sems.at[1]),
    ]
    for copy in copies:
        copy.start()
    for copy in copies:
        copy.wait()


def shards(data):
    rows, colsum = make_table()
    f32, bf16 = jnp.float32, jnp.bfloat16
    dma = pltpu.SemaphoreType.DMA
    vmem = pltpu.VMEM
    rfac, modes = pl.pallas_call(
        functools.partial(main_kernel, [float(v) for v in colsum]),
        out_shape=(vmem((F, 128, 128), f32), vmem((F, 128, PTS), f32)),
        in_specs=[pl.BlockSpec(memory_space=pltpu.HBM), pl.BlockSpec(memory_space=pltpu.HBM)],
        out_specs=[pl.BlockSpec(memory_space=pltpu.VMEM), pl.BlockSpec(memory_space=pltpu.VMEM)],
        scratch_shapes=[
            vmem((48, NFFT), f32),
            pltpu.SMEM((2 * F,), f32),
            vmem((CHUNKS, NT // NTM, CW), bf16),
            vmem((NTM, 2 * F * LB, PTS), f32),
            vmem((F, 2 * LB, COLS), bf16),
            vmem((2, 2 * NB, COLS), bf16),
            vmem((NTM, 8, 128), f32),
            vmem((2 * NB, COLS), f32),
            vmem((2, 16, 8, 128), f32),
            vmem((NSPACE, 8, 128), f32),
            vmem((16, 8, 128), f32),
            vmem((16, 8, 128), f32),
            vmem((F, 16, 8, 128), f32),
            vmem((F, 2, NTM, LB, PTS), f32),
            dma,
            dma((CHUNKS,)),
            dma((3,)),
            dma((2,)),
            dma((2,)),
            dma((2,)),
            dma((2,)),
            dma,
            dma((2, 7)),
            dma,
            dma((2, 8)),
            dma,
            pltpu.SemaphoreType.REGULAR,
            pltpu.SemaphoreType.REGULAR,
        ],
        compiler_params=pltpu.CompilerParams(
            collective_id=0, has_side_effects=True, vmem_limit_bytes=56 * 1024 * 1024
        ),
        name="factors",
    )(data, jnp.asarray(rows.astype(np.float32)))
    return pl.pallas_call(
        hand_out,
        out_shape=(
            jax.ShapeDtypeStruct((F, 128, 128), f32),
            jax.ShapeDtypeStruct((F, 128, PTS), f32),
        ),
        in_specs=[pl.BlockSpec(memory_space=pltpu.VMEM), pl.BlockSpec(memory_space=pltpu.VMEM)],
        out_specs=[pl.BlockSpec(memory_space=pl.ANY), pl.BlockSpec(memory_space=pl.ANY)],
        scratch_shapes=[dma((2,))],
        compiler_params=pltpu.CompilerParams(vmem_limit_bytes=8 * 1024 * 1024),
        name="hand_out",
    )(rfac, modes)


def solution(mesh):
    return jax.shard_map(
        shards,
        mesh=mesh,
        in_specs=(P("tm", "space"),),
        out_specs=(P(), P(None, None, ("space", "tm"))),
        check_vma=False,
    )
```

```python
import functools

import jax
import jax.numpy as jnp
import ml_dtypes
import numpy as np
from jax import lax
from jax.experimental import pallas as pl
from jax.experimental.pallas import tpu as pltpu
from jax.sharding import PartitionSpec as P

NFFT = 256
NB = 64
F = 16
NT = 16384
NX = 32768
NTM = 8
NSPACE = 32
LB = NB // NTM
COLS = NX // NSPACE
PTS = COLS // NTM
CHUNKS = 4
CW = COLS // CHUNKS
MESH = pl.DeviceIdType.MESH


def make_table():
    steps = np.arange(NFFT)
    window = 0.5 - 0.5 * np.cos(2.0 * np.pi * steps / NFFT)
    factor = 1.0 / np.sqrt(np.sum(window * window))
    freqs = np.arange(1, F + 1)
    phases = (steps[:, None] * freqs[None, :] % NFFT) * (2.0 * np.pi / NFFT)
    real = np.cos(phases) * (factor * window)[:, None]
    imag = -np.sin(phases) * (factor * window)[:, None]
    pairs = np.stack([real.T, imag.T], axis=1).reshape(2 * F, NFFT)
    rounded = pairs.astype(np.float32).astype(ml_dtypes.bfloat16)
    colsum = rounded.astype(np.float32).sum(axis=1, dtype=np.float32)
    rows = np.zeros((48, NFFT), ml_dtypes.bfloat16)
    rows[: 2 * F] = rounded
    rows[2 * F] = 1.0
    return rows, colsum


def factor(gt_ref, w_ref, half_done):
    lane = lax.broadcasted_iota(jnp.int32, (8, 128), 1)
    sub = lax.broadcasted_iota(jnp.int32, (8, 128), 0)
    for j in range(16):
        w_ref[j] = gt_ref[j]
    for k in range(16):
        base = 8 * k
        own = w_ref[k]
        cols = [jnp.broadcast_to(own[:, base + i : base + i + 1], (8, 128)) for i in range(8)]
        pivot_rows, inverses, cross = [], [], []
        diag = jnp.ones((8, 128), jnp.float32)
        for i in range(8):
            d = jnp.broadcast_to(cols[i][i : i + 1, :], (8, 128))
            inv = 1.0 / d
            row = jnp.broadcast_to(own[i : i + 1, :], (8, 128))
            diag = jnp.where(sub == i, d, diag)
            f = cols[i] * inv
            here = [jnp.broadcast_to(cols[m][i : i + 1, :], (8, 128)) for m in range(i + 1, 8)]
            for n, m in enumerate(range(i + 1, 8)):
                cols[m] = cols[m] - f * here[n]
            unit = jnp.where(lane == base + i, 1.0, row)
            own = jnp.where((lane == base + i) & (sub > i), 0.0, own) - jnp.where(
                sub > i, f, 0.0
            ) * unit
            pivot_rows.append(jnp.where((lane > base + i) & (lane < base + 8), 0.0, unit))
            inverses.append(inv)
            cross.append(here)
        w_ref[k] = own * lax.rsqrt(diag)
        if k == 11:
            half_done()
        for j in range(k + 1, 16):
            rest = w_ref[j]
            mult = [jnp.broadcast_to(rest[:, base + i : base + i + 1], (8, 128)) for i in range(8)]
            rest = jnp.where((lane >= base) & (lane < base + 8), 0.0, rest)
            for i in range(8):
                f = mult[i] * inverses[i]
                for n, m in enumerate(range(i + 1, 8)):
                    mult[m] = mult[m] - f * cross[i][n]
                rest = rest - f * pivot_rows[i]
            w_ref[j] = rest


def plane_distance(dz, dx):
    return min(dz, 8 - dz) + min(dx, 4 - dx)


PLANE = sorted(
    [(dz, dx) for dz in range(8) for dx in range(4) if dz or dx],
    key=lambda o: -plane_distance(*o),
)
OFFSET_Y = (1, 3, 2, 0, 1, 3, 2)
PARTS = ((0, 12), (12, 4))
HALF = [o for o in PLANE if sum(o) % 2 == 0]
OTHER = [o for o in PLANE if sum(o) % 2 == 1]
GROUP = [(2, 0), (2, 1), (1, 0), (3, 0), (1, 1), (3, 1), (0, 1)]


def main_kernel(
    colsum,
    data, tab_hbm, rfac, modes,
    tab, cs, dbuf, spec, sb, rb, ls, mat, gs, gr, gt, w, wa, mf,
    tab_sem, load_sem, fs_sem, ls_sem, ps_sem, ga_sem, gb_sem,
    w_ssem, w_rsem, r_ssem, r_rsem, own_sem, group_in, plane_in,
):
    t = lax.axis_index("tm")
    s = lax.axis_index("space")
    y, core = t // 2, t % 2
    z, x = s // 4, s % 4
    h = (x + z) % 2
    tile = z * 2 + x // 2
    sibling = 2 * y + 1 - core

    load_tab = pltpu.make_async_copy(tab_hbm, tab, tab_sem)
    load_tab.start()
    loads = []
    for c in range(CHUNKS):
        copy = pltpu.make_async_copy(
            data.at[:, pl.ds(c * CW, CW)], dbuf.at[c], load_sem.at[c]
        )
        copy.start()
        loads.append(copy)

    def remote(src, dst, send_sem, recv_sem, device):
        return pltpu.make_async_remote_copy(
            src_ref=src,
            dst_ref=dst,
            send_sem=send_sem,
            recv_sem=recv_sem,
            device_id=device,
            device_id_type=MESH,
        )

    def group_peer(o):
        return ((y + o[0]) % 4) * 2 + (core + o[1]) % 2

    def group_source(o):
        return ((y + 4 - o[0]) % 4) * 2 + (core + o[1]) % 2

    def plane_peer(o):
        return ((z + o[0]) % 8) * 4 + (x + o[1]) % 4

    barrier = pltpu.get_barrier_semaphore()

    def signal(sem, device):
        pl.semaphore_signal(sem, inc=1, device_id=device, device_id_type=MESH)

    for dy in (2, 1, 3, 0):
        other = ((y + dy) % 4) * 2
        if dy == 0:

            @pl.when(core == 1)
            def _():
                signal(barrier, (other, s))

        else:
            signal(barrier, (other, s))

    for j in range(2 * F):
        cs[j] = jnp.float32(colsum[j])
    load_tab.wait()
    table = tab[...].astype(jnp.bfloat16)

    for c in range(CHUNKS):
        cols = pl.ds(c * CW, CW)
        loads[c].wait()
        total = jnp.zeros((1, CW), jnp.float32)
        for b in range(LB):
            out = jnp.dot(
                table, dbuf[c, pl.ds(b * NFFT, NFFT), :], preferred_element_type=jnp.float32
            )
            for r in range(CW // 128):
                spec[c * (CW // 128) + r, pl.ds(b, 2 * F, stride=LB), :] = out[
                    : 2 * F, r * 128 : (r + 1) * 128
                ]
            total = total + out[2 * F : 2 * F + 1]
        for r in range(CW // 128):
            ls[t, pl.ds(c * (CW // 128) + r, 1), :] = total[:, r * 128 : (r + 1) * 128]
        local_mean = jnp.broadcast_to(total * (NTM / NT), (LB, CW))
        for r in range(CW // 128):
            place = c * (CW // 128) + r
            for f in range(F):
                parts = [
                    spec[place, pl.ds(f * 16 + ri * 8, 8), :]
                    - colsum[2 * f + ri] * local_mean[:, r * 128 : (r + 1) * 128]
                    for ri in range(2)
                ]
                sb[f, :, pl.ds(place * 128, 128)] = jnp.concatenate(parts, axis=0).astype(
                    jnp.bfloat16
                )

    @pl.when(core == 0)
    def _():
        pl.semaphore_wait(barrier, len(GROUP))
        signal(group_in, (sibling, s))

    @pl.when(core == 1)
    def _():
        pl.semaphore_wait(group_in, 1)

    def all_of(ref, send_sem, recv_sem):
        return remote(ref, ref, send_sem, recv_sem, (sibling, s))

    for o in GROUP:
        remote(ls.at[t], ls.at[t], ls_sem.at[0], ls_sem.at[1], (group_peer(o), s)).start()
    for f2 in range(2):
        for o in GROUP:
            other = group_peer(o)
            remote(
                sb.at[2 * other + f2],
                rb.at[f2, pl.ds(pl.multiple_of(t * 16, 16), 16), :],
                fs_sem.at[0],
                fs_sem.at[1 + f2],
                (other, s),
            ).start()

    @pl.when(core == 1)
    def _():
        for o in PLANE:
            signal(barrier, (t, plane_peer(o)))

    for f2 in range(2):
        rb[f2, pl.ds(pl.multiple_of(t * 16, 16), 16), :] = sb[2 * t + f2]

    sums_done = all_of(ls.at[pl.ds(0, 7)], ls_sem.at[0], ls_sem.at[1])
    sums_done.wait_recv()
    mean = ls[0]
    for k in range(1, NTM):
        mean = mean + ls[k]
    mean = mean * (1.0 / NT)

    def subtract(f, carry):
        for ri in range(2):
            rows = pl.ds(pl.multiple_of(f * 16 + ri * 8, 8), 8)
            for r in range(8):
                spec[r, rows, :] = spec[r, rows, :] - cs[2 * f + ri] * mean[r : r + 1, :]
        return carry

    lax.fori_loop(0, F, subtract, 0)
    spec5 = spec.reshape(NTM, F, 2, LB, PTS)

    for f2 in range(2):
        all_of(rb.at[f2, pl.ds(0, 7 * 16)], fs_sem.at[0], fs_sem.at[1 + f2]).wait_recv()
        real, imag = cs[4 * t + 2 * f2], cs[4 * t + 2 * f2 + 1]

        def gather(k, carry):
            for r in range(8):
                lanes = pl.ds(r * 128, 128)
                pieces = []
                for n in range(2):
                    source = 2 * k + n
                    shift = ls[source, pl.ds(r, 1), :] * (NTM / NT) - mean[r : r + 1, :]
                    block = rb[f2, pl.ds(pl.multiple_of(source * 16, 16), 16), lanes]
                    block = block.astype(jnp.float32)
                    pieces.append((block[:8] + real * shift, block[8:] + imag * shift))
                for part in range(2):
                    mat[pl.ds(pl.multiple_of(part * 64 + k * 16, 16), 16), lanes] = jnp.concatenate(
                        [piece[part] for piece in pieces], axis=0
                    ).astype(jnp.bfloat16)
            return carry

        lax.fori_loop(0, NTM // 2, gather, 0)
        rounded = mat[...]
        gram = lax.dot_general(
            rounded, rounded, (((1,), (1,)), ((), ())), preferred_element_type=jnp.float32
        ) * (1.0 / NX)
        for i in range(16):
            gs[f2, i] = gram[i * 8 : (i + 1) * 8]

        if f2 == 0:

            @pl.when(core == 1)
            def _():
                pl.semaphore_wait(barrier, len(PLANE))
                signal(plane_in, (sibling, s))

            @pl.when(core == 0)
            def _():
                pl.semaphore_wait(plane_in, 1)

        change = (h + f2) % 2

        def choose(a, b):
            return jnp.where(change == 0, a, b)

        def send_rows(i):
            keep = HALF[min(i, len(HALF) - 1)]
            oz = (z + choose(keep[0], OTHER[i][0])) % 8
            ox = (x + choose(keep[1], OTHER[i][1])) % 4
            k = choose(PLANE.index(keep), PLANE.index(OTHER[i]))
            remote(
                gs.at[f2, oz * 2 + ox // 2],
                gr.at[k],
                ga_sem.at[0],
                ga_sem.at[1],
                (t, oz * 4 + ox),
            ).start()

        for i in range(len(HALF)):
            send_rows(i)

        @pl.when(change == 1)
        def _():
            send_rows(len(HALF))

        if f2 == 1:
            for o in GROUP:
                other = group_peer(o)
                remote(
                    spec5.at[other], mf.at[:, :, t], ps_sem.at[0], ps_sem.at[1], (other, s)
                ).start()
            own_points = pltpu.make_async_copy(spec5.at[t], mf.at[:, :, t], own_sem)
            own_points.start()

    rows = gs[h, tile]
    rows_done = all_of(gr.at[pl.ds(0, len(PLANE))], ga_sem.at[0], ga_sem.at[1])
    rows_done.wait_recv()
    for i in range(len(PLANE)):
        rows = rows + gr[i]
    gt[tile] = rows

    for o in HALF:
        remote(gt.at[tile], gt.at[tile], gb_sem.at[0], gb_sem.at[1], (t, plane_peer(o))).start()
    tiles_done = all_of(gt.at[pl.ds(0, len(HALF))], gb_sem.at[0], gb_sem.at[1])
    tiles_done.wait_recv()

    mine = 2 * t + h

    def send_half(part):
        half_rows = pl.ds(*PARTS[part])
        for slot in (2, 1, 0, 6, 5, 4, 3):
            dy = OFFSET_Y[slot]
            other_y = (y + dy) % 4
            if slot < 3:
                column = s
            else:
                d = (y + other_y) % 4
                dx = jnp.where(d == 0, 1, jnp.where(d == 1, 3, 0))
                dz = jnp.where(d == 2, 1, jnp.where(d == 3, 7, 0))
                column = ((z + dz) % 8) * 4 + (x + dx) % 4
            remote(
                w.at[half_rows],
                wa.at[mine, half_rows],
                w_ssem,
                w_rsem.at[part, slot],
                (other_y * 2 + core, column),
            ).start()
        remote(
            w.at[half_rows], wa.at[mine, half_rows], r_ssem, r_rsem.at[part, 7], (sibling, s)
        ).start()

    factor(gt, w, lambda: send_half(0))
    send_half(1)
    own_points.wait()
    points_done = all_of(mf.at[:, :, pl.ds(0, 7)], ps_sem.at[0], ps_sem.at[1])
    points_done.wait_recv()
    row = lax.broadcasted_iota(jnp.int32, (128, 128), 0)
    col = lax.broadcasted_iota(jnp.int32, (128, 128), 1)

    def multiply(f, packed):
        packed = packed.reshape(128, 128)
        rfac[f] = jnp.where(col >= row, packed, 0.0)
        inverse = jnp.where(col < row, packed, jnp.where(col == row, 1.0 / packed, 0.0))
        modes[f] = jnp.dot(
            inverse,
            mf[f].reshape(128, PTS),
            preferred_element_type=jnp.float32,
            precision=lax.Precision.HIGH,
        )

    multiply(mine, w[...])
    order = [(i + 3 * h) % 7 for i in range(7)]

    def frequency(slot, of_core):
        turn = slot % 7
        dy = jnp.where(
            turn < 3,
            jnp.where(turn == 2, 2, 1 + 2 * turn),
            jnp.where(turn == 6, 2, jnp.where(turn == 5, 3, turn - 3)),
        )
        half = jnp.where(turn < 3, h, 1 - h)
        return 4 * ((y + 4 - dy) % 4) + 2 * of_core + half

    def relay(slot, part):
        f = frequency(slot, core)
        half_rows = wa.at[f, pl.ds(*PARTS[part])]
        remote(half_rows, half_rows, w_ssem, w_rsem.at[part, slot], (sibling, s)).wait_recv()
        remote(half_rows, half_rows, r_ssem, r_rsem.at[part, slot], (sibling, s)).start()

    for slots in (order[:3], order[3:]):
        for slot in slots:
            relay(slot, 0)
        for slot in slots:
            relay(slot, 1)
        for slot in slots:
            f = frequency(slot, core)
            multiply(f, wa[f])
    for i in range(8):
        slot = order[i - 1] if i else 7
        f = frequency(slot, 1 - core) if i else 4 * y + 2 * (1 - core) + h
        for part in range(2):
            half_rows = wa.at[f, pl.ds(*PARTS[part])]
            remote(half_rows, half_rows, r_ssem, r_rsem.at[part, slot], (sibling, s)).wait_recv()
        multiply(f, wa[f])

    for done in (sums_done, rows_done, tiles_done, points_done):
        done.wait_send()
    all_of(sb.at[pl.ds(0, 14)], fs_sem.at[0], fs_sem.at[1]).wait_send()
    all_of(wa.at[pl.ds(0, 7)], w_ssem, w_ssem).wait_send()
    all_of(wa.at[pl.ds(0, 8)], r_ssem, r_ssem).wait_send()


def hand_out(rfac, modes, rfac_out, modes_out, sems):
    copies = [
        pltpu.make_async_copy(rfac, rfac_out, sems.at[0]),
        pltpu.make_async_copy(modes, modes_out, sems.at[1]),
    ]
    for copy in copies:
        copy.start()
    for copy in copies:
        copy.wait()


def shards(data):
    rows, colsum = make_table()
    f32, bf16 = jnp.float32, jnp.bfloat16
    dma = pltpu.SemaphoreType.DMA
    vmem = pltpu.VMEM
    rfac, modes = pl.pallas_call(
        functools.partial(main_kernel, [float(v) for v in colsum]),
        out_shape=(vmem((F, 128, 128), f32), vmem((F, 128, PTS), f32)),
        in_specs=[pl.BlockSpec(memory_space=pltpu.HBM), pl.BlockSpec(memory_space=pltpu.HBM)],
        out_specs=[pl.BlockSpec(memory_space=pltpu.VMEM), pl.BlockSpec(memory_space=pltpu.VMEM)],
        scratch_shapes=[
            vmem((48, NFFT), f32),
            pltpu.SMEM((2 * F,), f32),
            vmem((CHUNKS, NT // NTM, CW), bf16),
            vmem((NTM, 2 * F * LB, PTS), f32),
            vmem((F, 2 * LB, COLS), bf16),
            vmem((2, 2 * NB, COLS), bf16),
            vmem((NTM, 8, 128), f32),
            vmem((2 * NB, COLS), bf16),
            vmem((2, 16, 8, 128), f32),
            vmem((NSPACE, 8, 128), f32),
            vmem((16, 8, 128), f32),
            vmem((16, 8, 128), f32),
            vmem((F, 16, 8, 128), f32),
            vmem((F, 2, NTM, LB, PTS), f32),
            dma,
            dma((CHUNKS,)),
            dma((3,)),
            dma((2,)),
            dma((2,)),
            dma((2,)),
            dma((2,)),
            dma,
            dma((2, 7)),
            dma,
            dma((2, 8)),
            dma,
            pltpu.SemaphoreType.REGULAR,
            pltpu.SemaphoreType.REGULAR,
        ],
        compiler_params=pltpu.CompilerParams(
            collective_id=0, has_side_effects=True, vmem_limit_bytes=56 * 1024 * 1024
        ),
        name="factors",
    )(data, jnp.asarray(rows.astype(np.float32)))
    return pl.pallas_call(
        hand_out,
        out_shape=(
            jax.ShapeDtypeStruct((F, 128, 128), f32),
            jax.ShapeDtypeStruct((F, 128, PTS), f32),
        ),
        in_specs=[pl.BlockSpec(memory_space=pltpu.VMEM), pl.BlockSpec(memory_space=pltpu.VMEM)],
        out_specs=[pl.BlockSpec(memory_space=pl.ANY), pl.BlockSpec(memory_space=pl.ANY)],
        scratch_shapes=[dma((2,))],
        compiler_params=pltpu.CompilerParams(vmem_limit_bytes=8 * 1024 * 1024),
        name="hand_out",
    )(rfac, modes)


def solution(mesh):
    return jax.shard_map(
        shards,
        mesh=mesh,
        in_specs=(P("tm", "space"),),
        out_specs=(P(), P(None, None, ("space", "tm"))),
        check_vma=False,
    )
```

```python
import functools

import jax
import jax.numpy as jnp
import ml_dtypes
import numpy as np
from jax import lax
from jax.experimental import pallas as pl
from jax.experimental.pallas import tpu as pltpu
from jax.sharding import PartitionSpec as P

NFFT = 256
NB = 64
F = 16
NT = 16384
NX = 32768
NTM = 8
NSPACE = 32
LB = NB // NTM
COLS = NX // NSPACE
PTS = COLS // NTM
CHUNKS = 4
CW = COLS // CHUNKS
MESH = pl.DeviceIdType.MESH


def make_table():
    steps = np.arange(NFFT)
    window = 0.5 - 0.5 * np.cos(2.0 * np.pi * steps / NFFT)
    factor = 1.0 / np.sqrt(np.sum(window * window))
    freqs = np.arange(1, F + 1)
    phases = (steps[:, None] * freqs[None, :] % NFFT) * (2.0 * np.pi / NFFT)
    real = np.cos(phases) * (factor * window)[:, None]
    imag = -np.sin(phases) * (factor * window)[:, None]
    pairs = np.stack([real.T, imag.T], axis=1).reshape(2 * F, NFFT)
    rounded = pairs.astype(np.float32).astype(ml_dtypes.bfloat16)
    colsum = rounded.astype(np.float32).sum(axis=1, dtype=np.float32)
    rows = np.zeros((48, NFFT), ml_dtypes.bfloat16)
    rows[: 2 * F] = rounded
    rows[2 * F] = 1.0
    return rows, colsum


def factor(gt_ref, w_ref, half_done):
    lane = lax.broadcasted_iota(jnp.int32, (8, 128), 1)
    sub = lax.broadcasted_iota(jnp.int32, (8, 128), 0)
    for j in range(16):
        w_ref[j] = gt_ref[j]
    for k in range(16):
        base = 8 * k
        own = w_ref[k]
        cols = [jnp.broadcast_to(own[:, base + i : base + i + 1], (8, 128)) for i in range(8)]
        pivot_rows, inverses, cross = [], [], []
        diag = jnp.ones((8, 128), jnp.float32)
        for i in range(8):
            d = jnp.broadcast_to(cols[i][i : i + 1, :], (8, 128))
            inv = 1.0 / d
            row = jnp.broadcast_to(own[i : i + 1, :], (8, 128))
            diag = jnp.where(sub == i, d, diag)
            f = cols[i] * inv
            here = [jnp.broadcast_to(cols[m][i : i + 1, :], (8, 128)) for m in range(i + 1, 8)]
            for n, m in enumerate(range(i + 1, 8)):
                cols[m] = cols[m] - f * here[n]
            unit = jnp.where(lane == base + i, 1.0, row)
            own = jnp.where((lane == base + i) & (sub > i), 0.0, own) - jnp.where(
                sub > i, f, 0.0
            ) * unit
            pivot_rows.append(jnp.where((lane > base + i) & (lane < base + 8), 0.0, unit))
            inverses.append(inv)
            cross.append(here)
        w_ref[k] = own * lax.rsqrt(diag)
        if k == 11:
            half_done()
        for j in range(k + 1, 16):
            rest = w_ref[j]
            mult = [jnp.broadcast_to(rest[:, base + i : base + i + 1], (8, 128)) for i in range(8)]
            rest = jnp.where((lane >= base) & (lane < base + 8), 0.0, rest)
            for i in range(8):
                f = mult[i] * inverses[i]
                for n, m in enumerate(range(i + 1, 8)):
                    mult[m] = mult[m] - f * cross[i][n]
                rest = rest - f * pivot_rows[i]
            w_ref[j] = rest


def plane_distance(dz, dx):
    return min(dz, 8 - dz) + min(dx, 4 - dx)


PLANE = sorted(
    [(dz, dx) for dz in range(8) for dx in range(4) if dz or dx],
    key=lambda o: -plane_distance(*o),
)
OFFSET_Y = (1, 3, 2, 0, 1, 3, 2)
PARTS = ((0, 12), (12, 4))
HALF = [o for o in PLANE if sum(o) % 2 == 0]
OTHER = [o for o in PLANE if sum(o) % 2 == 1]
GROUP = [(2, 0), (2, 1), (1, 0), (3, 0), (1, 1), (3, 1), (0, 1)]


def main_kernel(
    colsum,
    data, tab_hbm, rfac, modes,
    tab, cs, dbuf, spec, sb, rb, ls, mat, gs, gr, gt, w, wa, mf,
    tab_sem, load_sem, fs_sem, ls_sem, ps_sem, ga_sem, gb_sem,
    w_ssem, w_rsem, r_ssem, r_rsem, own_sem, group_in, plane_in,
):
    t = lax.axis_index("tm")
    s = lax.axis_index("space")
    y, core = t // 2, t % 2
    z, x = s // 4, s % 4
    h = (x + z) % 2
    tile = z * 2 + x // 2
    sibling = 2 * y + 1 - core

    def remote(src, dst, send_sem, recv_sem, device):
        return pltpu.make_async_remote_copy(
            src_ref=src,
            dst_ref=dst,
            send_sem=send_sem,
            recv_sem=recv_sem,
            device_id=device,
            device_id_type=MESH,
        )

    def group_peer(o):
        return ((y + o[0]) % 4) * 2 + (core + o[1]) % 2

    def group_source(o):
        return ((y + 4 - o[0]) % 4) * 2 + (core + o[1]) % 2

    def plane_peer(o):
        return ((z + o[0]) % 8) * 4 + (x + o[1]) % 4

    barrier = pltpu.get_barrier_semaphore()

    def signal(sem, device):
        pl.semaphore_signal(sem, inc=1, device_id=device, device_id_type=MESH)

    for dy in (2, 1, 3, 0):
        other = ((y + dy) % 4) * 2
        if dy == 0:

            @pl.when(core == 1)
            def _():
                signal(barrier, (other, s))

        else:
            signal(barrier, (other, s))

    load_tab = pltpu.make_async_copy(tab_hbm, tab, tab_sem)
    load_tab.start()
    loads = []
    for c in range(CHUNKS):
        copy = pltpu.make_async_copy(
            data.at[:, pl.ds(c * CW, CW)], dbuf.at[c], load_sem.at[c]
        )
        copy.start()
        loads.append(copy)

    for j in range(2 * F):
        cs[j] = jnp.float32(colsum[j])
    load_tab.wait()
    table = tab[...].astype(jnp.bfloat16)

    for c in range(CHUNKS):
        cols = pl.ds(c * CW, CW)
        loads[c].wait()
        total = jnp.zeros((1, CW), jnp.float32)
        for b in range(LB):
            out = jnp.dot(
                table, dbuf[c, pl.ds(b * NFFT, NFFT), :], preferred_element_type=jnp.float32
            )
            for r in range(CW // 128):
                spec[c * (CW // 128) + r, pl.ds(b, 2 * F, stride=LB), :] = out[
                    : 2 * F, r * 128 : (r + 1) * 128
                ]
            total = total + out[2 * F : 2 * F + 1]
        for r in range(CW // 128):
            ls[t, pl.ds(c * (CW // 128) + r, 1), :] = total[:, r * 128 : (r + 1) * 128]
        local_mean = jnp.broadcast_to(total * (NTM / NT), (LB, CW))
        for r in range(CW // 128):
            place = c * (CW // 128) + r
            for f in range(F):
                parts = [
                    spec[place, pl.ds(f * 16 + ri * 8, 8), :]
                    - colsum[2 * f + ri] * local_mean[:, r * 128 : (r + 1) * 128]
                    for ri in range(2)
                ]
                sb[f, :, pl.ds(place * 128, 128)] = jnp.concatenate(parts, axis=0).astype(
                    jnp.bfloat16
                )

    @pl.when(core == 0)
    def _():
        pl.semaphore_wait(barrier, len(GROUP))
        signal(group_in, (sibling, s))

    @pl.when(core == 1)
    def _():
        pl.semaphore_wait(group_in, 1)

    def all_of(ref, send_sem, recv_sem):
        return remote(ref, ref, send_sem, recv_sem, (sibling, s))

    for o in GROUP:
        remote(ls.at[t], ls.at[t], ls_sem.at[0], ls_sem.at[1], (group_peer(o), s)).start()
    for f2 in range(2):
        for o in GROUP:
            other = group_peer(o)
            remote(
                sb.at[2 * other + f2],
                rb.at[f2, pl.ds(pl.multiple_of(t * 16, 16), 16), :],
                fs_sem.at[0],
                fs_sem.at[1 + f2],
                (other, s),
            ).start()

    @pl.when(core == 1)
    def _():
        for o in PLANE:
            signal(barrier, (t, plane_peer(o)))

    for f2 in range(2):
        rb[f2, pl.ds(pl.multiple_of(t * 16, 16), 16), :] = sb[2 * t + f2]

    sums_done = all_of(ls.at[pl.ds(0, 7)], ls_sem.at[0], ls_sem.at[1])
    sums_done.wait_recv()
    mean = ls[0]
    for k in range(1, NTM):
        mean = mean + ls[k]
    mean = mean * (1.0 / NT)

    def subtract(f, carry):
        for ri in range(2):
            rows = pl.ds(pl.multiple_of(f * 16 + ri * 8, 8), 8)
            for r in range(8):
                spec[r, rows, :] = spec[r, rows, :] - cs[2 * f + ri] * mean[r : r + 1, :]
        return carry

    lax.fori_loop(0, F, subtract, 0)
    spec5 = spec.reshape(NTM, F, 2, LB, PTS)

    for f2 in range(2):
        all_of(rb.at[f2, pl.ds(0, 7 * 16)], fs_sem.at[0], fs_sem.at[1 + f2]).wait_recv()
        real, imag = cs[4 * t + 2 * f2], cs[4 * t + 2 * f2 + 1]

        def gather(k, carry):
            for r in range(8):
                lanes = pl.ds(r * 128, 128)
                pieces = []
                for n in range(2):
                    source = 2 * k + n
                    shift = ls[source, pl.ds(r, 1), :] * (NTM / NT) - mean[r : r + 1, :]
                    block = rb[f2, pl.ds(pl.multiple_of(source * 16, 16), 16), lanes]
                    block = block.astype(jnp.float32)
                    pieces.append((block[:8] + real * shift, block[8:] + imag * shift))
                for part in range(2):
                    mat[pl.ds(pl.multiple_of(part * 64 + k * 16, 16), 16), lanes] = jnp.concatenate(
                        [piece[part] for piece in pieces], axis=0
                    ).astype(jnp.bfloat16)
            return carry

        lax.fori_loop(0, NTM // 2, gather, 0)
        rounded = mat[...]
        gram = lax.dot_general(
            rounded, rounded, (((1,), (1,)), ((), ())), preferred_element_type=jnp.float32
        ) * (1.0 / NX)
        for i in range(16):
            gs[f2, i] = gram[i * 8 : (i + 1) * 8]

        if f2 == 0:

            @pl.when(core == 1)
            def _():
                pl.semaphore_wait(barrier, len(PLANE))
                signal(plane_in, (sibling, s))

            @pl.when(core == 0)
            def _():
                pl.semaphore_wait(plane_in, 1)

        change = (h + f2) % 2

        def choose(a, b):
            return jnp.where(change == 0, a, b)

        def send_rows(i):
            keep = HALF[min(i, len(HALF) - 1)]
            oz = (z + choose(keep[0], OTHER[i][0])) % 8
            ox = (x + choose(keep[1], OTHER[i][1])) % 4
            k = choose(PLANE.index(keep), PLANE.index(OTHER[i]))
            remote(
                gs.at[f2, oz * 2 + ox // 2],
                gr.at[k],
                ga_sem.at[0],
                ga_sem.at[1],
                (t, oz * 4 + ox),
            ).start()

        for i in range(len(HALF)):
            send_rows(i)

        @pl.when(change == 1)
        def _():
            send_rows(len(HALF))

        if f2 == 1:
            for o in GROUP:
                other = group_peer(o)
                remote(
                    spec5.at[other], mf.at[:, :, t], ps_sem.at[0], ps_sem.at[1], (other, s)
                ).start()
            own_points = pltpu.make_async_copy(spec5.at[t], mf.at[:, :, t], own_sem)
            own_points.start()

    rows = gs[h, tile]
    rows_done = all_of(gr.at[pl.ds(0, len(PLANE))], ga_sem.at[0], ga_sem.at[1])
    rows_done.wait_recv()
    for i in range(len(PLANE)):
        rows = rows + gr[i]
    gt[tile] = rows

    for o in HALF:
        remote(gt.at[tile], gt.at[tile], gb_sem.at[0], gb_sem.at[1], (t, plane_peer(o))).start()
    tiles_done = all_of(gt.at[pl.ds(0, len(HALF))], gb_sem.at[0], gb_sem.at[1])
    tiles_done.wait_recv()

    mine = 2 * t + h

    def send_half(part):
        half_rows = pl.ds(*PARTS[part])
        for slot in (6, 2, 5, 4, 1, 0, 3):
            dy = OFFSET_Y[slot]
            other_y = (y + dy) % 4
            if slot < 3:
                column = s
            else:
                d = (y + other_y) % 4
                dx = jnp.where(d == 0, 1, jnp.where(d == 1, 3, 0))
                dz = jnp.where(d == 2, 1, jnp.where(d == 3, 7, 0))
                column = ((z + dz) % 8) * 4 + (x + dx) % 4
            remote(
                w.at[half_rows],
                wa.at[mine, half_rows],
                w_ssem,
                w_rsem.at[part, slot],
                (other_y * 2 + core, column),
            ).start()
        remote(
            w.at[half_rows], wa.at[mine, half_rows], r_ssem, r_rsem.at[part, 7], (sibling, s)
        ).start()

    factor(gt, w, lambda: send_half(0))
    send_half(1)
    own_points.wait()
    points_done = all_of(mf.at[:, :, pl.ds(0, 7)], ps_sem.at[0], ps_sem.at[1])
    points_done.wait_recv()
    row = lax.broadcasted_iota(jnp.int32, (128, 128), 0)
    col = lax.broadcasted_iota(jnp.int32, (128, 128), 1)

    def multiply(f, packed):
        packed = packed.reshape(128, 128)
        rfac[f] = jnp.where(col >= row, packed, 0.0)
        inverse = jnp.where(col < row, packed, jnp.where(col == row, 1.0 / packed, 0.0))
        modes[f] = jnp.dot(
            inverse,
            mf[f].reshape(128, PTS),
            preferred_element_type=jnp.float32,
            precision=lax.Precision.HIGH,
        )

    multiply(mine, w[...])
    order = [(i + 3 * h) % 7 for i in range(7)]

    def frequency(slot, of_core):
        turn = slot % 7
        dy = jnp.where(
            turn < 3,
            jnp.where(turn == 2, 2, 1 + 2 * turn),
            jnp.where(turn == 6, 2, jnp.where(turn == 5, 3, turn - 3)),
        )
        half = jnp.where(turn < 3, h, 1 - h)
        return 4 * ((y + 4 - dy) % 4) + 2 * of_core + half

    def relay(slot, part):
        f = frequency(slot, core)
        half_rows = wa.at[f, pl.ds(*PARTS[part])]
        remote(half_rows, half_rows, w_ssem, w_rsem.at[part, slot], (sibling, s)).wait_recv()
        remote(half_rows, half_rows, r_ssem, r_rsem.at[part, slot], (sibling, s)).start()

    for slots in (order[:3], order[3:]):
        for slot in slots:
            relay(slot, 0)
        for slot in slots:
            relay(slot, 1)
        for slot in slots:
            f = frequency(slot, core)
            multiply(f, wa[f])
    for i in range(8):
        slot = order[i - 1] if i else 7
        f = frequency(slot, 1 - core) if i else 4 * y + 2 * (1 - core) + h
        for part in range(2):
            half_rows = wa.at[f, pl.ds(*PARTS[part])]
            remote(half_rows, half_rows, r_ssem, r_rsem.at[part, slot], (sibling, s)).wait_recv()
        multiply(f, wa[f])

    for done in (sums_done, rows_done, tiles_done, points_done):
        done.wait_send()
    all_of(sb.at[pl.ds(0, 14)], fs_sem.at[0], fs_sem.at[1]).wait_send()
    all_of(wa.at[pl.ds(0, 7)], w_ssem, w_ssem).wait_send()
    all_of(wa.at[pl.ds(0, 8)], r_ssem, r_ssem).wait_send()


def hand_out(rfac, modes, rfac_out, modes_out, sems):
    copies = [
        pltpu.make_async_copy(rfac, rfac_out, sems.at[0]),
        pltpu.make_async_copy(modes, modes_out, sems.at[1]),
    ]
    for copy in copies:
        copy.start()
    for copy in copies:
        copy.wait()


def shards(data):
    rows, colsum = make_table()
    f32, bf16 = jnp.float32, jnp.bfloat16
    dma = pltpu.SemaphoreType.DMA
    vmem = pltpu.VMEM
    rfac, modes = pl.pallas_call(
        functools.partial(main_kernel, [float(v) for v in colsum]),
        out_shape=(vmem((F, 128, 128), f32), vmem((F, 128, PTS), f32)),
        in_specs=[pl.BlockSpec(memory_space=pltpu.HBM), pl.BlockSpec(memory_space=pltpu.HBM)],
        out_specs=[pl.BlockSpec(memory_space=pltpu.VMEM), pl.BlockSpec(memory_space=pltpu.VMEM)],
        scratch_shapes=[
            vmem((48, NFFT), f32),
            pltpu.SMEM((2 * F,), f32),
            vmem((CHUNKS, NT // NTM, CW), bf16),
            vmem((NTM, 2 * F * LB, PTS), f32),
            vmem((F, 2 * LB, COLS), bf16),
            vmem((2, 2 * NB, COLS), bf16),
            vmem((NTM, 8, 128), f32),
            vmem((2 * NB, COLS), bf16),
            vmem((2, 16, 8, 128), f32),
            vmem((NSPACE, 8, 128), f32),
            vmem((16, 8, 128), f32),
            vmem((16, 8, 128), f32),
            vmem((F, 16, 8, 128), f32),
            vmem((F, 2, NTM, LB, PTS), f32),
            dma,
            dma((CHUNKS,)),
            dma((3,)),
            dma((2,)),
            dma((2,)),
            dma((2,)),
            dma((2,)),
            dma,
            dma((2, 7)),
            dma,
            dma((2, 8)),
            dma,
            pltpu.SemaphoreType.REGULAR,
            pltpu.SemaphoreType.REGULAR,
        ],
        compiler_params=pltpu.CompilerParams(
            collective_id=0, has_side_effects=True, vmem_limit_bytes=56 * 1024 * 1024
        ),
        name="factors",
    )(data, jnp.asarray(rows.astype(np.float32)))
    return pl.pallas_call(
        hand_out,
        out_shape=(
            jax.ShapeDtypeStruct((F, 128, 128), f32),
            jax.ShapeDtypeStruct((F, 128, PTS), f32),
        ),
        in_specs=[pl.BlockSpec(memory_space=pltpu.VMEM), pl.BlockSpec(memory_space=pltpu.VMEM)],
        out_specs=[pl.BlockSpec(memory_space=pl.ANY), pl.BlockSpec(memory_space=pl.ANY)],
        scratch_shapes=[dma((2,))],
        compiler_params=pltpu.CompilerParams(vmem_limit_bytes=8 * 1024 * 1024),
        name="hand_out",
    )(rfac, modes)


def solution(mesh):
    return jax.shard_map(
        shards,
        mesh=mesh,
        in_specs=(P("tm", "space"),),
        out_specs=(P(), P(None, None, ("space", "tm"))),
        check_vma=False,
    )
```
